128 devices in a mesh: pipe: 2 (over core), dp: 16 (over y, x), tensor: 4 (over z).
Axes of the slice: x: 4, y: 4, z: 4, core: 2. Of those that a mesh axis runs over, the one named last changes fastest.
Arguments:
- saved_inputs: bfloat16 [2, 2, 2, 6144, 896], P('pipe', None, None, 'dp')
- early_cotangents: bfloat16 [2, 2, 6144, 896], P('pipe', None, 'dp'), may hold values from -30 to 30
- final_cotangent: bfloat16 [6144, 896], P('dp'), may hold values from -6 to 6
- valid_counts: int32 [16, 2], P('dp'), may hold values from 96 to 384, as said below
- master: float32 [2, 896, 2, 3, 2560], P('pipe', 'dp', None, None, 'tensor'), may hold values from -0.1875 to 0.1875
- first_moment: bfloat16 [2, 896, 2, 3, 2560], P('pipe', 'dp', None, None, 'tensor'), may hold values from -6 to 6
- second_moment: bfloat16 [2, 896, 2, 3, 2560], P('pipe', 'dp', None, None, 'tensor'), may hold values from 0.049804688 to 5
Outputs:
- new_master: float32 [2, 896, 2, 3, 2560], P('pipe', 'dp', None, None, 'tensor')
- new_first: bfloat16 [2, 896, 2, 3, 2560], P('pipe', 'dp', None, None, 'tensor')
- new_second: bfloat16 [2, 896, 2, 3, 2560], P('pipe', 'dp', None, None, 'tensor')
The draws below stay inside these ranges and needn't reach their ends.
Inputs may be any that keep to these rules, and one draw needn't show every extreme that they name: `valid_counts`: every draw has an entry equal to 384.
All inputs are finite; a program needn't handle non-finite values.
Results may differ from the reference program's by a relative error of at most 0.025.
Values may be sent and summed in bfloat16 or wider, within the bound.
No kernel may reach another device: no remote copies, remote signals or barrier semaphores. Data moves between devices by JAX's collectives and lax.ppermute only.
A program may use at most 448 MiB of HBM per device.

```python
import math
import jax
import jax.numpy as jnp
from jax import lax

D = 896
FF = 2560
MB_TOK = 384
STEP = 20
TOKENS = 6144
PARAMS = 27525120
N_PIPE = 2
N_DP = 16
N_TENSOR = 4


def replicate_blocks(block, axis_index):
    reps = [1] * block.ndim
    reps[axis_index] = N_DP
    return jnp.tile(block, tuple(reps))


def draw_saved_inputs(key, part):
    key = jax.random.fold_in(key, 11)
    own_key, shared_key, row_key, column_key = jax.random.split(key, 4)
    shape_all = (N_PIPE, 2, 2, TOKENS, D)
    shape_block = (N_PIPE, 2, 2, MB_TOK, D)
    own_part = jax.random.normal(own_key, shape_all, jnp.float32)
    shared_part = jax.random.normal(shared_key, shape_block, jnp.float32)
    shared_weight = 0.6
    own_weight = 0.8
    ramp_slope = 2.0
    standard = shared_weight * replicate_blocks(shared_part, 3) + own_weight * own_part
    row_scale = jnp.exp(jax.random.uniform(row_key, (N_PIPE, 2, 2, TOKENS, 1), jnp.float32, math.log(0.15), math.log(0.6)))
    column_scale = jnp.exp(jax.random.uniform(column_key, (N_PIPE, 2, 1, 1, D), jnp.float32, math.log(0.3), math.log(3.0)))
    column_ramp = 1.0 + ramp_slope * jnp.arange(D, dtype=jnp.float32) / (D - 1)
    return (standard * row_scale * column_scale * column_ramp).astype(jnp.bfloat16)


def draw_early_cotangents(key, part):
    key = jax.random.fold_in(key, 37)
    own_key, shared_key = jax.random.split(key)
    shape_all = (N_PIPE, 2, TOKENS, D)
    shape_block = (N_PIPE, 2, MB_TOK, D)
    own_part = jnp.clip(jax.random.normal(own_key, shape_all, jnp.float32), -6.0, 6.0)
    shared_part = jnp.clip(jax.random.normal(shared_key, shape_block, jnp.float32), -6.0, 6.0)
    shared_weight = 0.6
    own_weight = 0.8
    peak = 3.0
    standard = shared_weight * replicate_blocks(shared_part, 2) + own_weight * own_part
    section_scale = peak - (peak - 1.0) * jnp.arange(N_PIPE, dtype=jnp.float32) / (N_PIPE - 1)
    return (standard * section_scale[:, None, None, None]).astype(jnp.bfloat16)


def draw_final_cotangent(key, part):
    key = jax.random.fold_in(key, 53)
    own_key, shared_key = jax.random.split(key)
    own_part = jax.random.normal(own_key, (TOKENS, D), jnp.float32)
    shared_part = jax.random.normal(shared_key, (MB_TOK, D), jnp.float32)
    shared_weight = 0.6
    own_weight = 0.8
    standard = shared_weight * replicate_blocks(shared_part, 0) + own_weight * own_part
    return jnp.clip(standard, -6.0, 6.0).astype(jnp.bfloat16)


def draw_valid_counts(key, part):
    key = jax.random.fold_in(key, 23)
    count_key, slot_key = jax.random.split(key)
    counts = jax.random.randint(count_key, (N_DP, 2), MB_TOK // 4, MB_TOK + 1)
    chosen_slot = jax.random.randint(slot_key, (), 0, 2 * N_DP)
    flat_index = jnp.arange(2 * N_DP, dtype=jnp.int32).reshape(N_DP, 2)
    return jnp.where(flat_index == chosen_slot, MB_TOK, counts).astype(jnp.int32)


def steps_of(stream_key, shape, cuts, smallest, largest):
    factor_of = 1.0
    for axis_at, shards_of in cuts:
        draws = jax.random.uniform(jax.random.fold_in(jax.random.fold_in(stream_key, 6), axis_at), (shards_of,), jnp.float32, smallest / len(cuts), largest / len(cuts))
        factor_of = factor_of * jnp.repeat(jnp.exp(draws), shape[axis_at] // shards_of).reshape((-1,) + (1,) * (len(shape) - 1 - axis_at))
    return factor_of


def noise(rng, extent, width, limit, cuts=(), held_as=jnp.bfloat16):
    entries = width * jax.random.normal(rng, extent, jnp.float32)
    if cuts:
        entries = entries * steps_of(rng, extent, cuts, -0.22, 0.18)
    return jnp.clip(entries, -limit, limit).astype(held_as)


def setup_inputs(seed: int = 0) -> dict:
    splits = jax.random.split(jax.random.key(seed), 8)
    saved_inputs = draw_saved_inputs(jax.random.fold_in(splits[7], 71), 0)
    early_cotangents = draw_early_cotangents(jax.random.fold_in(splits[7], 71), 0)
    final_cotangent = draw_final_cotangent(jax.random.fold_in(splits[7], 71), 0)
    valid_counts = draw_valid_counts(jax.random.fold_in(splits[7], 71), 0)
    master = noise(splits[4], (N_PIPE, D, 2, 3, FF), D ** -0.5, 0.1875, ((0, 2), (1, 16), (4, 4)), jnp.float32)
    first_moment = noise(splits[5], (N_PIPE, D, 2, 3, FF), 1.0, 6.0, ((0, 2), (1, 16), (4, 4)))
    second_moment = jnp.clip(jnp.exp(math.log(5.0) - 4.609084 * jax.random.uniform(splits[6], (N_PIPE, D, 2, 3, FF), jnp.float32) ** steps_of(splits[6], (N_PIPE, D, 2, 3, FF), ((0, 2), (1, 16), (4, 4)), -0.2, 0.2)), 0.049804688, 5.0).astype(jnp.bfloat16)
    return {"saved_inputs": saved_inputs, "early_cotangents": early_cotangents, "final_cotangent": final_cotangent, "valid_counts": valid_counts, "master": master, "first_moment": first_moment, "second_moment": second_moment}


def normalize_rows(inputs):
    values = inputs.astype(jnp.float32)
    root_mean = jnp.sqrt(lax.optimization_barrier(jnp.mean(values * values, axis=-1, keepdims=True)) + 1e-06)
    unit_rows = values / root_mean
    return (unit_rows, root_mean, unit_rows.astype(jnp.bfloat16))

def hidden_pass(normed, cotangent, w_gate, w_up, w_down):
    gate = jnp.dot(normed, w_gate, preferred_element_type=jnp.float32)
    up_rows = jnp.dot(normed, w_up, preferred_element_type=jnp.float32)
    sigmoid_gate = jax.nn.sigmoid(gate)
    activated = gate * sigmoid_gate
    hidden = (activated * up_rows).astype(jnp.bfloat16)
    hidden_grad = jnp.dot(cotangent, w_down, preferred_element_type=jnp.float32)
    grad_gate = (hidden_grad * up_rows * sigmoid_gate * (1.0 + gate * (1.0 - sigmoid_gate))).astype(jnp.bfloat16)
    grad_up = (hidden_grad * activated).astype(jnp.bfloat16)
    return (hidden, grad_gate, grad_up)

def branch_rows(unit_rows, root_mean, grad_gate, grad_up, w_gate, w_up):
    contract = (((1,), (1,)), ((), ()))
    branch = lax.dot_general(grad_gate, w_gate, contract, preferred_element_type=jnp.float32)
    branch = branch + lax.dot_general(grad_up, w_up, contract, preferred_element_type=jnp.float32)
    centered = branch - unit_rows * lax.optimization_barrier(jnp.mean(branch * unit_rows, axis=-1, keepdims=True))
    return (centered / root_mean).astype(jnp.bfloat16)

def accumulate(running, item):
    inputs_rows, grad_rows, cot_rows, hidden_rows = item
    term_rows = jnp.concatenate([jnp.dot(inputs_rows.T, grad_rows, preferred_element_type=jnp.float32), jnp.dot(cot_rows.T, hidden_rows, preferred_element_type=jnp.float32)], axis=1)
    rounded = lax.optimization_barrier(term_rows.astype(jnp.bfloat16))
    return (running + rounded.astype(running.dtype), None)

def reference(saved_inputs, early_cotangents, final_cotangent, valid_counts, master, first_moment, second_moment):
    weights = master.astype(jnp.bfloat16)
    group = FF // N_TENSOR
    token_index = jnp.arange(TOKENS, dtype=jnp.int32)
    replica = token_index // MB_TOK
    offset_in = token_index % MB_TOK
    live_early = (offset_in < valid_counts[replica, 0])[:, None]
    live_last = (offset_in < valid_counts[replica, 1])[:, None]

    def matrices(section_index, leg_index):
        return (weights[section_index, :, leg_index, 0, :], weights[section_index, :, leg_index, 1, :], weights[section_index, :, leg_index, 2, :])

    def layer_pass(section_index, leg_index, micro, cotangent, with_branch):
        w_gate, w_up, w_down = matrices(section_index, leg_index)
        unit_rows, root_mean, normed = normalize_rows(saved_inputs[section_index, leg_index, micro])
        hidden, grad_gate, grad_up = hidden_pass(normed, cotangent, w_gate, w_up, w_down)
        if not with_branch:
            return (normed, hidden, grad_gate, grad_up, None)
        running = cotangent.astype(jnp.float32)
        for group_index in range(N_TENSOR):
            lower = group_index * group
            upper = lower + group
            part_rows = branch_rows(unit_rows, root_mean, grad_gate[:, lower:upper], grad_up[:, lower:upper], w_gate[:, lower:upper], w_up[:, lower:upper])
            running = running + part_rows.astype(jnp.float32)
        return (normed, hidden, grad_gate, grad_up, running.astype(jnp.bfloat16))
    cotangent = jnp.where(live_last, final_cotangent, 0).astype(jnp.bfloat16)
    stored = {}
    for layer_index in range(2 * N_PIPE - 1, -1, -1):
        if layer_index >= N_PIPE:
            section_index, leg_index = (2 * N_PIPE - 1 - layer_index, 1)
        else:
            section_index, leg_index = (layer_index, 0)
        normed, hidden, grad_gate, grad_up, next_cot = layer_pass(section_index, leg_index, 1, cotangent, layer_index > 0)
        stored[section_index, leg_index] = (normed, hidden, grad_gate, grad_up, cotangent)
        cotangent = next_cot

    def split_rows(early_rows, last_rows):
        return jnp.concatenate([early_rows.reshape(N_DP, MB_TOK, -1), last_rows.reshape(N_DP, MB_TOK, -1)], axis=1)
    section_grads = []
    for section_index in range(N_PIPE):
        leg_grads = []
        for leg_index in range(2):
            normed_last, hidden_last, gate_last, up_last, cot_last = stored[section_index, leg_index]
            cot_early = jnp.where(live_early, early_cotangents[section_index, leg_index], 0).astype(jnp.bfloat16)
            normed_early, hidden_early, gate_early, up_early, unused = layer_pass(section_index, leg_index, 0, cot_early, False)
            inputs_rows = split_rows(normed_early, normed_last)
            grad_rows = split_rows(jnp.concatenate([gate_early, up_early], 1), jnp.concatenate([gate_last, up_last], 1))
            cot_rows = split_rows(cot_early, cot_last)
            hidden_rows = split_rows(hidden_early, hidden_last)
            summed, unused_out = lax.scan(accumulate, jnp.zeros((D, 3 * FF), jnp.float32), (inputs_rows, grad_rows, cot_rows, hidden_rows))
            leg_grads.append(summed.reshape(D, 3, FF))
        section_grads.append(jnp.stack(leg_grads, axis=1))
    gradient = jnp.stack(section_grads, axis=0)
    total = jnp.sum(gradient * gradient)
    clip_factor = jnp.minimum(1.0, math.sqrt(PARAMS) / (jnp.sqrt(total) + 1e-06))
    scaled = gradient * clip_factor
    moment_one = 0.9 * first_moment.astype(jnp.float32) + 0.1 * scaled
    moment_two = 0.95 * second_moment.astype(jnp.float32) + 0.05 * scaled * scaled
    update = moment_one / (1.0 - 0.9 ** STEP) / (jnp.sqrt(moment_two / (1.0 - 0.95 ** STEP)) + 1e-08) + 0.1 * master
    new_master = master - 0.001 * update
    return (new_master, moment_one.astype(jnp.bfloat16), moment_two.astype(jnp.bfloat16))
```

```python
import math

import jax
import jax.numpy as jnp
from jax import lax
from jax.sharding import PartitionSpec as P

STEP = 20
SIDE = 4
CUT = 1024
F32 = jnp.float32
BF16 = jnp.bfloat16


def from_x(value, by):
    pairs = [
        (y * SIDE + (x + by) % SIDE, y * SIDE + x) for y in range(SIDE) for x in range(SIDE)
    ]
    return lax.ppermute(value, "dp", pairs)


def from_y(value, by):
    pairs = [
        (((y + by) % SIDE) * SIDE + x, y * SIDE + x) for y in range(SIDE) for x in range(SIDE)
    ]
    return lax.ppermute(value, "dp", pairs)


def from_z(value, by, source, target):
    pairs = [(source * SIDE + (z + by) % SIDE, target * SIDE + z) for z in range(SIDE)]
    return lax.ppermute(value, ("pipe", "tensor"), pairs)


ORDER = (2, 1, 3)


def peers(fetch):
    got = {by: fetch(by) for by in ORDER}
    return [got[by] for by in (1, 2, 3)]


def gather_rows(shard):
    first, second = shard[:, :CUT], shard[:, CUT:]
    first_x = jnp.stack([first] + peers(lambda by: from_x(first, by)), 0)
    second_y = jnp.stack([second] + peers(lambda by: from_y(second, by)), 0)
    first_all = jnp.stack([first_x] + peers(lambda by: from_y(first_x, by)), 0)
    second_all = jnp.stack([second_y] + peers(lambda by: from_x(second_y, by)), 1)
    whole = jnp.concatenate([first_all, second_all], axis=-1)
    return whole.reshape(-1, whole.shape[-1])


def total_of(parts):
    total = parts[0].astype(F32)
    for part in parts[1:]:
        total = total + part.astype(F32)
    return total


def scatter_rows(first, second):
    first_y = total_of([first[0]] + peers(lambda by: from_y(first[by], -by)))
    second_x = total_of([second[:, 0]] + peers(lambda by: from_x(second[:, by], -by)))
    first_y16, second_x16 = first_y.astype(BF16), second_x.astype(BF16)
    first_own = total_of([first_y[0]] + peers(lambda by: from_x(first_y16[by], -by)))
    second_own = total_of([second_x[0]] + peers(lambda by: from_y(second_x16[by], -by)))
    return first_own, second_own


def normalize_rows(inputs):
    values = inputs.astype(F32)
    root_mean = jnp.sqrt(jnp.mean(values * values, axis=-1, keepdims=True) + 1e-06)
    unit_rows = values / root_mean
    return (unit_rows, root_mean, unit_rows.astype(BF16))


def gate_pass(normed, weights, units):
    gate = jnp.dot(normed, weights[:, :units], preferred_element_type=F32)
    up_rows = jnp.dot(normed, weights[:, units : 2 * units], preferred_element_type=F32)
    sigmoid_gate = jax.nn.sigmoid(gate)
    activated = gate * sigmoid_gate
    hidden = (activated * up_rows).astype(BF16)
    slope = up_rows * sigmoid_gate * (1.0 + gate * (1.0 - sigmoid_gate))
    return hidden, slope, activated


def back_pass(cotangent, slope, activated, weights, units):
    hidden_grad = jnp.dot(cotangent, weights[:, 2 * units :], preferred_element_type=F32)
    return (hidden_grad * slope).astype(BF16), (hidden_grad * activated).astype(BF16)


def branch_rows(unit_rows, root_mean, grad_gate, grad_up, weights, units):
    contract = (((1,), (1,)), ((), ()))
    branch = lax.dot_general(grad_gate, weights[:, :units], contract, preferred_element_type=F32)
    branch = branch + lax.dot_general(
        grad_up, weights[:, units : 2 * units], contract, preferred_element_type=F32
    )
    centered = branch - unit_rows * jnp.mean(branch * unit_rows, axis=-1, keepdims=True)
    return (centered / root_mean).astype(BF16)


def next_cotangent(cotangent, part_rows, source, target):
    groups = part_rows.reshape(SIDE, -1, part_rows.shape[-1])
    mine = total_of(
        [groups[0]] + peers(lambda by: from_z(groups[by], -by, source, source))
    )
    mine = (cotangent[: groups.shape[1]].astype(F32) + mine).astype(BF16)
    own = mine if source == target else from_z(mine, 0, source, target)
    return jnp.concatenate([own] + peers(lambda by: from_z(mine, by, source, target)), 0)


def summed_everywhere(value):
    value = jnp.broadcast_to(value, (8, 128))
    value = value + lax.ppermute(value, "pipe", [(0, 1), (1, 0)])
    value = total_of([value] + peers(lambda by: from_x(value, by)))
    value = total_of([value] + peers(lambda by: from_y(value, by)))
    rounds = [
        lax.ppermute(value, "tensor", [((z + by) % SIDE, z) for z in range(SIDE)]) for by in ORDER
    ]
    return total_of([value] + rounds)[0, 0]


def per_device(
    saved_inputs,
    early_cotangents,
    final_cotangent,
    valid_counts,
    master,
    first_moment,
    second_moment,
):
    row_count, width = saved_inputs.shape[3:]
    units = master.shape[4]
    share = width // lax.axis_size("dp")
    section = lax.axis_index("pipe")
    place = lax.axis_index("dp")
    place_y, place_x = place // SIDE, place % SIDE
    place_z = lax.axis_index("tensor")
    group = row_count // SIDE

    shards = master[0].astype(BF16).reshape(share, 2, 3 * units)
    upper_weights = gather_rows(shards[:, 1])
    lower_shard, _ = lax.optimization_barrier((shards[:, 0], upper_weights))
    lower_weights = gather_rows(lower_shard)

    block = jnp.arange(width) // share
    source_block = ((place_y + block // SIDE) % SIDE) * SIDE + (place_x + block % SIDE) % SIDE
    source_column = source_block * share + jnp.arange(width) % share
    mover = (jnp.arange(width)[:, None] == source_column[None, :]).astype(BF16)
    turns = [(place_z + j) % SIDE for j in range(SIDE)]

    def turned(rows):
        return jnp.concatenate(
            [lax.dynamic_slice_in_dim(rows, turn * group, group, rows.ndim - 2) for turn in turns],
            rows.ndim - 2,
        )

    def moved(rows):
        return jnp.dot(turned(rows), mover, preferred_element_type=F32).astype(BF16)

    inputs = moved(saved_inputs[0])
    position = turned(lax.broadcasted_iota(jnp.int32, (row_count, 1), 0))
    early = jnp.where(position < valid_counts[0, 0], moved(early_cotangents[0]), 0)
    final = jnp.where(position < valid_counts[0, 1], moved(final_cotangent), 0)

    unit1, root1, normed1 = normalize_rows(inputs[1, 1])
    hidden1, slope1, active1 = gate_pass(normed1, upper_weights, units)
    gate3, up3 = back_pass(final, slope1, active1, upper_weights, units)
    part3 = branch_rows(unit1, root1, gate3, up3, upper_weights, units)
    cot2 = next_cotangent(final, part3, 0, 1)
    cot_upper = jnp.where(section == 0, final, cot2)
    gate1, up1 = back_pass(cot_upper, slope1, active1, upper_weights, units)
    part2 = branch_rows(unit1, root1, gate1, up1, upper_weights, units)
    cot1 = next_cotangent(cot_upper, part2, 1, 1)

    unit0, root0, normed0 = normalize_rows(inputs[0, 1])
    hidden0, slope0, active0 = gate_pass(normed0, lower_weights, units)
    gate_first, up_first = back_pass(cot1, slope0, active0, lower_weights, units)
    part1 = branch_rows(unit0, root0, gate_first, up_first, lower_weights, units)
    cot0 = next_cotangent(cot1, part1, 1, 0)
    cot_lower = jnp.where(section == 1, cot1, cot0)
    gate0, up0 = back_pass(cot_lower, slope0, active0, lower_weights, units)

    def leg_terms(leg, weights, normed_last, cot_last, gate_last, up_last, hidden_last):
        _, _, normed_early = normalize_rows(inputs[leg, 0])
        hidden_early, slope, activated = gate_pass(normed_early, weights, units)
        gate_early, up_early = back_pass(early[leg], slope, activated, weights, units)
        normed = jnp.concatenate([normed_early, normed_last], 0)
        grads = jnp.concatenate(
            [
                jnp.concatenate([gate_early, up_early], 1),
                jnp.concatenate([gate_last, up_last], 1),
            ],
            0,
        )
        cot = jnp.concatenate([early[leg], cot_last], 0)
        hidden = jnp.concatenate([hidden_early, hidden_last], 0)

        def term(left, right):
            return jnp.einsum("td,tf->df", left, right, preferred_element_type=F32).astype(BF16)

        first = term(normed, grads[:, :CUT])
        second = jnp.concatenate([term(normed, grads[:, CUT:]), term(cot, hidden)], 1)
        parts = [t.reshape(SIDE, SIDE, share, -1) for t in (first, second)]
        return jnp.concatenate(scatter_rows(*parts), -1)

    upper_gradient = leg_terms(1, upper_weights, normed1, cot_upper, gate1, up1, hidden1)
    lower_gradient = leg_terms(0, lower_weights, normed0, cot_lower, gate0, up0, hidden0)
    gradient = jnp.stack([lower_gradient, upper_gradient], 1).reshape(1, share, 2, 3, units)

    total = summed_everywhere(jnp.sum(gradient * gradient))
    param_count = lax.axis_size("pipe") * 6 * width * units * lax.axis_size("tensor")
    clip_factor = jnp.minimum(1.0, math.sqrt(param_count) / (jnp.sqrt(total) + 1e-06))
    scaled = gradient * clip_factor
    moment_one = 0.9 * first_moment.astype(F32) + 0.1 * scaled
    moment_two = 0.95 * second_moment.astype(F32) + 0.05 * scaled * scaled
    update = (
        moment_one / (1.0 - 0.9**STEP) / (jnp.sqrt(moment_two / (1.0 - 0.95**STEP)) + 1e-08)
        + 0.1 * master
    )
    new_master = master - 0.001 * update
    return (new_master, moment_one.astype(BF16), moment_two.astype(BF16))


def solution(mesh):
    in_specs = (
        P("pipe", None, None, "dp", None),
        P("pipe", None, "dp", None),
        P("dp", None),
        P("dp", None),
        P("pipe", "dp", None, None, "tensor"),
        P("pipe", "dp", None, None, "tensor"),
        P("pipe", "dp", None, None, "tensor"),
    )
    out_specs = (
        P("pipe", "dp", None, None, "tensor"),
        P("pipe", "dp", None, None, "tensor"),
        P("pipe", "dp", None, None, "tensor"),
    )
    return jax.shard_map(
        per_device, mesh=mesh, in_specs=in_specs, out_specs=out_specs, check_vma=False
    )
```

```python
import functools
import math

import jax
import jax.numpy as jnp
from jax import lax
from jax.experimental import pallas as pl
from jax.experimental.pallas import tpu as pltpu
from jax.sharding import PartitionSpec as P

STEP = 20
SIDE = 4
F32 = jnp.float32
BF16 = jnp.bfloat16
ORDER = (2, 1, 3)


def peers(fetch):
    got = {by: fetch(by) for by in ORDER}
    return [got[by] for by in (1, 2, 3)]


def from_plane(value, by, first):
    pairs = []
    for core in range(2):
        for y in range(SIDE):
            for x in range(SIDE):
                if (core == 0) == first:
                    source = (y, (x + by) % SIDE)
                else:
                    source = ((y + by) % SIDE, x)
                base = core * SIDE * SIDE
                pairs.append((base + source[0] * SIDE + source[1], base + y * SIDE + x))
    return lax.ppermute(value, ("pipe", "dp"), pairs)


def from_z(value, by, source, target):
    pairs = [(source * SIDE + (z + by) % SIDE, target * SIDE + z) for z in range(SIDE)]
    return lax.ppermute(value, ("pipe", "tensor"), pairs)


def gather_rows(shard):
    block = jnp.concatenate([shard] + peers(lambda by: from_plane(shard, by, True)), 0)
    return [block] + peers(lambda by: from_plane(block, by, False))


def total_of(parts):
    total = parts[0].astype(F32)
    for part in parts[1:]:
        total = total + part.astype(F32)
    return total


def run(kernel, ins, outs, scratch=(), flops=0, name=None):
    arrays, specs = [], []
    for item in ins:
        array, space = item if isinstance(item, tuple) else (item, pltpu.VMEM)
        arrays.append(array)
        specs.append(pl.BlockSpec(memory_space=space))
    moved = sum(a.size * a.dtype.itemsize for a in arrays)
    moved += sum(math.prod(s) * jnp.dtype(t).itemsize for s, t in outs)
    return pl.pallas_call(
        kernel,
        out_shape=[jax.ShapeDtypeStruct(s, t) for s, t in outs],
        in_specs=specs,
        out_specs=[pl.BlockSpec(memory_space=pltpu.VMEM)] * len(outs),
        scratch_shapes=list(scratch),
        compiler_params=pltpu.CompilerParams(vmem_limit_bytes=52 * 1024 * 1024),
        cost_estimate=pl.CostEstimate(flops=flops, bytes_accessed=moved, transcendentals=0),
        name=name,
    )(*arrays)


def weight_copies(pieces, weights, sems):
    rows = pieces[0].shape[0]
    return [
        pltpu.make_async_copy(piece, weights.at[pl.ds(i * rows, rows)], sems.at[i])
        for i, piece in enumerate(pieces)
    ]


def normalized(inputs):
    values = inputs.astype(F32)
    root_mean = jnp.sqrt(jnp.mean(values * values, axis=-1, keepdims=True) + 1e-06)
    return values / root_mean, root_mean


def dot(left, right):
    return jnp.dot(left, right, preferred_element_type=F32)


def gate_parts(normed, weights, units):
    both = dot(normed, weights[:, : 2 * units])
    gate, up_rows = both[:, :units], both[:, units:]
    sigmoid_gate = jax.nn.sigmoid(gate)
    activated = gate * sigmoid_gate
    hidden = (activated * up_rows).astype(BF16)
    slope = up_rows * sigmoid_gate * (1.0 + gate * (1.0 - sigmoid_gate))
    return hidden, slope, activated


def both_grads(cotangent, slope, activated, weights, units):
    hidden_grad = dot(cotangent, weights[:, 2 * units :])
    return jnp.concatenate(
        [(hidden_grad * slope).astype(BF16), (hidden_grad * activated).astype(BF16)], 1
    )


def store_branch(grads, inputs, weights, units, outs):
    branch = lax.dot_general(
        grads, weights[:, : 2 * units], (((1,), (1,)), ((), ())), preferred_element_type=F32
    )
    unit_rows, root_mean = normalized(inputs)
    centered = branch - unit_rows * jnp.mean(branch * unit_rows, axis=-1, keepdims=True)
    rows = (centered / root_mean).astype(BF16)
    group = rows.shape[0] // SIDE
    for i, out in enumerate(outs):
        out[...] = rows[i * group : (i + 1) * group]


def gate_kernel(units, x, *refs):
    pieces, outs, weights, sems = refs[:4], refs[4:8], refs[8], refs[9]
    copies = weight_copies(pieces, weights, sems)
    for copy in copies:
        copy.start()
    normed = normalized(x[...])[0].astype(BF16)
    outs[0][...] = normed.T
    for copy in copies:
        copy.wait()
    outs[1][...], outs[2][...], outs[3][...] = gate_parts(normed, weights, units)


def first_kernel(units, x, d, *refs):
    pieces, outs, weights, sems = refs[:4], refs[4:12], refs[12], refs[13]
    copies = weight_copies(pieces, weights, sems)
    for copy in copies:
        copy.start()
    normed = normalized(x[...])[0].astype(BF16)
    outs[0][...] = normed.T
    for copy in copies:
        copy.wait()
    hidden, slope, activated = gate_parts(normed, weights, units)
    outs[1][...], outs[2][...], outs[3][...] = hidden, slope, activated
    grads = both_grads(d[...], slope, activated, weights, units)
    store_branch(grads, x[...], weights, units, outs[4:])


def chain_kernel(units, x, slope, activated, *refs):
    groups, pieces, outs, weights, sems = refs[:4], refs[4:8], refs[8:12], refs[12], refs[13]
    copies = weight_copies(pieces, weights, sems)
    for copy in copies:
        copy.start()
    cotangent = jnp.concatenate([g[...] for g in groups], 0)
    for copy in copies:
        copy.wait()
    grads = both_grads(cotangent, slope[...], activated[...], weights, units)
    store_branch(grads, x[...], weights, units, outs)


def early_kernel(units, x, d, *refs):
    pieces, outs, weights, sems = refs[:4], refs[4:8], refs[8], refs[9]
    copies = weight_copies(pieces, weights, sems)
    for copy in copies:
        copy.start()
    normed = normalized(x[...])[0].astype(BF16)
    outs[0][...] = normed.T
    outs[1][...] = d[...].T
    for copy in copies:
        copy.wait()
    hidden, slope, activated = gate_parts(normed, weights, units)
    outs[2][...] = hidden
    outs[3][...] = both_grads(d[...], slope, activated, weights, units)


def terms_kernel(units, use_first, *refs):
    first, second = refs[:4], refs[4:8]
    normed_early, cot_early, hidden_early, grads_early = refs[8:12]
    normed_last, hidden_last, slope, activated = refs[12:16]
    pieces, outs = refs[16:20], refs[20:24]
    weights, sems, lefts, grads, hiddens = refs[24:]
    copies = weight_copies(pieces, weights, sems)
    for copy in copies:
        copy.start()
    tokens = normed_early.shape[1]
    cotangent = jnp.concatenate(
        [jnp.where(use_first[0] != 0, a[...], b[...]) for a, b in zip(first, second)], 0
    )
    lefts[0, :, :tokens] = normed_early[...]
    lefts[0, :, tokens:] = normed_last[...]
    lefts[1, :, :tokens] = cot_early[...]
    lefts[1, :, tokens:] = cotangent.T
    grads[:tokens] = grads_early[...]
    hiddens[:tokens] = hidden_early[...]
    hiddens[tokens:] = hidden_last[...]
    for copy in copies:
        copy.wait()
    grads[tokens:] = both_grads(cotangent, slope[...], activated[...], weights, units)
    for i, out in enumerate(outs):
        rows = slice(i * out.shape[0], (i + 1) * out.shape[0])
        out[:, : 2 * units] = dot(lefts[0, rows], grads[...]).astype(BF16)
        out[:, 2 * units :] = dot(lefts[1, rows], hiddens[...]).astype(BF16)


def mix_kernel(crossing, d, *refs):
    total = d[...].astype(F32) + total_of([r[...] for r in refs[:4]])
    rows = total.astype(BF16)
    if crossing:
        rows = dot(rows, refs[4][...]).astype(BF16)
    refs[-1][...] = rows


def add_kernel(*refs):
    total = total_of([r[...] for r in refs[:4]])
    outs = refs[4:]
    rows = total.shape[0] // len(outs)
    for i, out in enumerate(outs):
        out[...] = total[i * rows : (i + 1) * rows].astype(out.dtype)


def finish_kernel(*refs):
    total = total_of([r[...] for r in refs[:4]])
    refs[4][...] = total
    squares = jnp.sum(total * total, axis=0, keepdims=True)
    refs[5][...] = jnp.broadcast_to(jnp.sum(squares, axis=1, keepdims=True), refs[5].shape)


def scatter_rows(pieces):
    share, wide = pieces[0].shape[0] // SIDE, pieces[0].shape[1]
    parts = [pieces[0]] + peers(lambda by: from_plane(pieces[by], -by, False))
    sums = run(add_kernel, parts, [((share, wide), F32)] + [((share, wide), BF16)] * 3, name="add")
    parts = [sums[0]] + peers(lambda by: from_plane(sums[by], -by, True))
    return run(finish_kernel, parts, [((share, wide), F32), ((8, 128), F32)], name="finish")


def next_cotangent(first_group, parts, source, target, swap):
    got = [parts[0]] + peers(lambda by: from_z(parts[by], -by, source, source))
    crossing = source != target
    (mine,) = run(
        functools.partial(mix_kernel, crossing),
        [first_group] + got + ([swap] if crossing else []),
        [(first_group.shape, BF16)],
        name="mix",
    )
    rest = peers(lambda by: from_z(mine, by, source, target))
    own = from_z(mine, 0, source, target) if crossing else mine
    return [own] + rest


def summed_everywhere(value):
    value = value + lax.ppermute(value, "pipe", [(0, 1), (1, 0)])
    value = total_of([value] + peers(lambda by: from_plane(value, by, True)))
    value = total_of([value] + peers(lambda by: from_plane(value, by, False)))
    rounds = peers(
        lambda by: lax.ppermute(value, "tensor", [((z + by) % SIDE, z) for z in range(SIDE)])
    )
    return total_of([value] + rounds)[0, 0]


def per_device(
    saved_inputs,
    early_cotangents,
    final_cotangent,
    valid_counts,
    master,
    first_moment,
    second_moment,
):
    tokens, width = saved_inputs.shape[3:]
    units = master.shape[4]
    share = width // lax.axis_size("dp")
    section = lax.axis_index("pipe")
    place = lax.axis_index("dp")
    place_y, place_x = place // SIDE, place % SIDE
    place_z = lax.axis_index("tensor")
    group = tokens // SIDE
    wide = 3 * units

    shards = master[0].astype(BF16).reshape(share, 2, wide)
    upper = gather_rows(shards[:, 1])
    lower_shard, _ = lax.optimization_barrier((shards[:, 0], upper[0]))
    lower = gather_rows(lower_shard)

    block = jnp.arange(width) // share
    outer, inner = block // SIDE, block % SIDE
    by_y = jnp.where(section == 0, outer, inner)
    by_x = jnp.where(section == 0, inner, outer)
    source_block = ((place_y + by_y) % SIDE) * SIDE + (place_x + by_x) % SIDE
    source_column = source_block * share + jnp.arange(width) % share
    mover = (jnp.arange(width)[:, None] == source_column[None, :]).astype(BF16)
    swapped_column = (inner * SIDE + outer) * share + jnp.arange(width) % share
    swap = (jnp.arange(width)[:, None] == swapped_column[None, :]).astype(BF16)
    turns = [(place_z + j) % SIDE for j in range(SIDE)]

    def turned(rows):
        return jnp.concatenate(
            [lax.dynamic_slice_in_dim(rows, turn * group, group, rows.ndim - 2) for turn in turns],
            rows.ndim - 2,
        )

    def moved(rows):
        return jnp.dot(turned(rows), mover, preferred_element_type=F32).astype(BF16)

    inputs = moved(saved_inputs[0])
    position = turned(lax.broadcasted_iota(jnp.int32, (tokens, 1), 0))
    early = jnp.where(position < valid_counts[0, 0], moved(early_cotangents[0]), 0)
    final = jnp.where(position < valid_counts[0, 1], moved(final_cotangent), 0)
    final_groups = [final[i * group : (i + 1) * group] for i in range(SIDE)]

    flop = 2 * tokens * width * units
    weight_scratch = [pltpu.VMEM((width, wide), BF16), pltpu.SemaphoreType.DMA((SIDE,))]
    half_outs = [
        ((width, tokens), BF16),
        ((tokens, units), BF16),
        ((tokens, units), F32),
        ((tokens, units), F32),
    ]
    group_outs = [((group, width), BF16)] * SIDE

    def apart(pieces):
        return [(piece, pl.ANY) for piece in pieces]

    def chain(leg_inputs, half, groups, pieces):
        return run(
            functools.partial(chain_kernel, units),
            [leg_inputs, half[2], half[3], *groups, *apart(pieces)],
            group_outs,
            weight_scratch,
            3 * flop,
            "chain",
        )

    def early_parts(leg, pieces):
        return run(
            functools.partial(early_kernel, units),
            [inputs[leg, 0], early[leg], *apart(pieces)],
            [
                ((width, tokens), BF16),
                ((width, tokens), BF16),
                ((tokens, units), BF16),
                ((tokens, 2 * units), BF16),
            ],
            weight_scratch,
            3 * flop,
            "early",
        )

    def terms(use_first, first, second, early_half, half, pieces):
        return run(
            functools.partial(terms_kernel, units),
            [
                (use_first.astype(jnp.int32).reshape(1), pltpu.SMEM),
                *first,
                *second,
                *early_half,
                *half,
                *apart(pieces),
            ],
            [((width // SIDE, wide), BF16)] * SIDE,
            weight_scratch
            + [
                pltpu.VMEM((2, width, 2 * tokens), BF16),
                pltpu.VMEM((2 * tokens, 2 * units), BF16),
                pltpu.VMEM((2 * tokens, units), BF16),
            ],
            7 * flop,
            "terms",
        )

    outs = run(
        functools.partial(first_kernel, units),
        [inputs[1, 1], final, *apart(upper)],
        half_outs + group_outs,
        weight_scratch,
        5 * flop,
        "first",
    )
    upper_half, part3 = outs[:4], outs[4:]
    cot2 = next_cotangent(final_groups[0], part3, 0, 1, swap)
    part2 = chain(inputs[1, 1], upper_half, cot2, upper)
    cot1 = next_cotangent(cot2[0], part2, 1, 1, swap)

    lower_half = run(
        functools.partial(gate_kernel, units),
        [inputs[0, 1], *apart(lower)],
        half_outs,
        weight_scratch,
        2 * flop,
        "gate",
    )
    part1 = chain(inputs[0, 1], lower_half, cot1, lower)
    cot0 = next_cotangent(cot1[0], part1, 1, 0, swap)

    upper_terms = terms(section == 0, final_groups, cot2, early_parts(1, upper), upper_half, upper)
    upper_gradient, upper_squares = scatter_rows(upper_terms)
    lower_terms = terms(section == 1, cot1, cot0, early_parts(0, lower), lower_half, lower)
    lower_gradient, lower_squares = scatter_rows(lower_terms)
    gradient = jnp.stack([lower_gradient, upper_gradient], 1).reshape(1, share, 2, 3, units)

    total = summed_everywhere(lower_squares + upper_squares)
    param_count = lax.axis_size("pipe") * 6 * width * units * lax.axis_size("tensor")
    clip_factor = jnp.minimum(1.0, math.sqrt(param_count) / (jnp.sqrt(total) + 1e-06))
    scaled = gradient * clip_factor
    moment_one = 0.9 * first_moment.astype(F32) + 0.1 * scaled
    moment_two = 0.95 * second_moment.astype(F32) + 0.05 * scaled * scaled
    update = (
        moment_one / (1.0 - 0.9**STEP) / (jnp.sqrt(moment_two / (1.0 - 0.95**STEP)) + 1e-08)
        + 0.1 * master
    )
    new_master = master - 0.001 * update
    return (new_master, moment_one.astype(BF16), moment_two.astype(BF16))


def solution(mesh):
    in_specs = (
        P("pipe", None, None, "dp", None),
        P("pipe", None, "dp", None),
        P("dp", None),
        P("dp", None),
        P("pipe", "dp", None, None, "tensor"),
        P("pipe", "dp", None, None, "tensor"),
        P("pipe", "dp", None, None, "tensor"),
    )
    out_specs = (
        P("pipe", "dp", None, None, "tensor"),
        P("pipe", "dp", None, None, "tensor"),
        P("pipe", "dp", None, None, "tensor"),
    )
    return jax.shard_map(
        per_device, mesh=mesh, in_specs=in_specs, out_specs=out_specs, check_vma=False
    )
```

```python
import functools
import math

import jax
import jax.numpy as jnp
from jax import lax
from jax.experimental import pallas as pl
from jax.experimental.pallas import tpu as pltpu
from jax.sharding import PartitionSpec as P

STEP = 20
SIDE = 4
F32 = jnp.float32
BF16 = jnp.bfloat16
ORDER = (1, 3, 2)
VMEM_LIMIT = 20 * 1024 * 1024


def peers(fetch):
    got = {by: fetch(by) for by in ORDER}
    return [got[by] for by in (1, 2, 3)]


def from_plane(value, by, first):
    pairs = []
    for core in range(2):
        for y in range(SIDE):
            for x in range(SIDE):
                if (core == 0) == first:
                    source = (y, (x + by) % SIDE)
                else:
                    source = ((y + by) % SIDE, x)
                base = core * SIDE * SIDE
                pairs.append((base + source[0] * SIDE + source[1], base + y * SIDE + x))
    return lax.ppermute(value, ("pipe", "dp"), pairs)


def from_z(value, by):
    pairs = [((z + by) % SIDE, z) for z in range(SIDE)]
    return lax.ppermute(value, "tensor", pairs)


def across(value, by, source):
    pairs = [(source * SIDE + (z + by) % SIDE, (1 - source) * SIDE + z) for z in range(SIDE)]
    pairs += [((1 - source) * SIDE + z, source * SIDE + z) for z in range(SIDE)]
    return lax.ppermute(value, ("pipe", "tensor"), pairs)


def from_other_core(value):
    return lax.ppermute(value, "pipe", [(0, 1), (1, 0)])


def total_of(parts):
    total = parts[0].astype(F32)
    for part in parts[1:]:
        total = total + part.astype(F32)
    return total


def run(kernel, ins, outs, scratch=(), flops=0, name=None):
    arrays, specs = [], []
    for item in ins:
        array, space = item if isinstance(item, tuple) else (item, pltpu.VMEM)
        arrays.append(array)
        specs.append(pl.BlockSpec(memory_space=space))
    moved = sum(a.size * a.dtype.itemsize for a in arrays)
    moved += sum(math.prod(o[0]) * jnp.dtype(o[1]).itemsize for o in outs)
    return pl.pallas_call(
        kernel,
        out_shape=[jax.ShapeDtypeStruct(o[0], o[1]) for o in outs],
        in_specs=specs,
        out_specs=[pl.BlockSpec(memory_space=o[2] if o[2:] else pltpu.VMEM) for o in outs],
        scratch_shapes=list(scratch),
        compiler_params=pltpu.CompilerParams(vmem_limit_bytes=VMEM_LIMIT),
        cost_estimate=pl.CostEstimate(flops=flops, bytes_accessed=moved, transcendentals=0),
        name=name,
    )(*arrays)


def after(value, *others):
    return lax.optimization_barrier((value, others))[0]


def normalized(inputs):
    values = inputs.astype(F32)
    root_mean = jnp.sqrt(jnp.mean(values * values, axis=-1, keepdims=True) + 1e-06)
    return values / root_mean, root_mean


def dot(left, right):
    return jnp.dot(left, right, preferred_element_type=F32)


def gate_parts(normed, weights, units):
    both = dot(normed, weights[:, : 2 * units])
    gate, up_rows = both[:, :units], both[:, units:]
    sigmoid_gate = jax.nn.sigmoid(gate)
    activated = gate * sigmoid_gate
    hidden = (activated * up_rows).astype(BF16)
    slope = up_rows * sigmoid_gate * (1.0 + gate * (1.0 - sigmoid_gate))
    return hidden, slope, activated


def both_grads(cotangent, slope, activated, weights, units):
    hidden_grad = dot(cotangent, weights[:, 2 * units :])
    return jnp.concatenate(
        [(hidden_grad * slope).astype(BF16), (hidden_grad * activated).astype(BF16)], 1
    )


def store_branch(grads, inputs, weights, units, outs):
    branch = lax.dot_general(
        grads, weights[:, : 2 * units], (((1,), (1,)), ((), ())), preferred_element_type=F32
    )
    unit_rows, root_mean = normalized(inputs)
    centered = branch - unit_rows * jnp.mean(branch * unit_rows, axis=-1, keepdims=True)
    rows = (centered / root_mean).astype(BF16)
    group = rows.shape[0] // SIDE
    for i, out in enumerate(outs):
        out[...] = rows[i * group : (i + 1) * group]


def started(copies):
    for copy in copies:
        copy.start()
    return copies


def waited(copies):
    for copy in copies:
        copy.wait()


def weight_copies(pieces, weights, sems):
    rows, columns = pieces[0].shape[0], weights.shape[1]
    first = pieces[0].shape[1] - columns
    return started(
        [
            pltpu.make_async_copy(
                piece.at[:, pl.ds(first, columns)], weights.at[pl.ds(i * rows, rows)], sems.at[i]
            )
            for i, piece in enumerate(pieces)
        ]
    )


def order_kernel(mover, whole, out, matrix, weights, sems):
    rows, columns = out.shape[0] // SIDE, out.shape[1] // 3
    copies = [pltpu.make_async_copy(mover, matrix, sems.at[0])]
    for i in range(3):
        part = pl.ds(i * columns, columns)
        copies.append(
            pltpu.make_async_copy(whole.at[:, part], weights.at[:, part], sems.at[i + 1])
        )
    started(copies)
    copies[0].wait()
    for i in range(3):
        copies[i + 1].wait()
        part = slice(i * columns, (i + 1) * columns)
        out[:, part] = dot(matrix[...], weights[:, part]).astype(BF16)


def gate_kernel(units, x, weights, *outs):
    normed = normalized(x[...])[0].astype(BF16)
    outs[0][...] = normed.T
    outs[1][...], outs[2][...], outs[3][...] = gate_parts(normed, weights, units)


def first_kernel(units, x, d, *refs):
    pieces, halves, outs = refs[:4], refs[4:8], refs[8:12]
    weights, sems, stages, out_sems = refs[12], refs[13], refs[14:18], refs[18]
    copies = weight_copies(pieces, weights, sems)
    sends = [
        pltpu.make_async_copy(stage, half, out_sems.at[i])
        for i, (stage, half) in enumerate(zip(stages, halves))
    ]
    normed = normalized(x[...])[0].astype(BF16)
    stages[0][...] = normed.T
    sends[0].start()
    waited(copies)
    hidden, slope, activated = gate_parts(normed, weights, units)
    stages[1][...], stages[2][...], stages[3][...] = hidden, slope, activated
    started(sends[1:])
    grads = both_grads(d[...], slope, activated, weights, units)
    store_branch(grads, x[...], weights, units, outs)
    waited(sends)


def chain_kernel(units, active, x, slope, activated, weights, *refs):
    groups, outs = refs[:4], refs[4:]

    @pl.when(active[0] != 0)
    def _():
        cotangent = jnp.concatenate([g[...] for g in groups], 0)
        grads = both_grads(cotangent, slope[...], activated[...], weights, units)
        store_branch(grads, x[...], weights, units, outs)

    @pl.when(active[0] == 0)
    def _():
        for out in outs:
            out[...] = jnp.zeros(out.shape, out.dtype)


def far_chain_kernel(units, active, x, slope, activated, *refs):
    pieces, groups, outs = refs[:4], refs[4:8], refs[8:12]
    weights, sems, slope_here, activated_here = refs[12:]

    @pl.when(active[0] != 0)
    def _():
        copies = weight_copies(pieces, weights, sems)
        copies += started(
            [
                pltpu.make_async_copy(slope, slope_here, sems.at[4]),
                pltpu.make_async_copy(activated, activated_here, sems.at[5]),
            ]
        )
        cotangent = jnp.concatenate([g[...] for g in groups], 0)
        waited(copies)
        grads = both_grads(cotangent, slope_here[...], activated_here[...], weights, units)
        store_branch(grads, x[...], weights, units, outs)

    @pl.when(active[0] == 0)
    def _():
        for out in outs:
            out[...] = jnp.zeros(out.shape, out.dtype)


def early_kernel(units, x, d, *refs):
    if len(refs) > 5:
        pieces, outs, weights, sems = refs[:4], refs[4:8], refs[8], refs[9]
        copies = weight_copies(pieces, weights, sems)
    else:
        weights, outs, copies = refs[0], refs[1:], []
    normed = normalized(x[...])[0].astype(BF16)
    outs[0][...] = normed.T
    outs[1][...] = d[...].T
    waited(copies)
    hidden, slope, activated = gate_parts(normed, weights, units)
    outs[2][...] = hidden
    outs[3][...] = both_grads(d[...], slope, activated, weights, units)


def terms_kernel(units, use_first, *refs):
    first, second = refs[:4], refs[4:8]
    normed_early, cot_early, hidden_early, grads_early = refs[8:12]
    normed_last, hidden_last, slope, activated = refs[12:16]
    lefts, grads, hiddens = refs[-3:]
    if len(refs) > 24:
        pieces, outs, weights, sems = refs[16:20], refs[20:24], refs[24], refs[25]
        copies = weight_copies(pieces, weights, sems)
    else:
        weights, outs, copies = refs[16], refs[17:21], []
    down = slice(weights.shape[1] - units, weights.shape[1])
    tokens = normed_early.shape[1]
    cotangent = jnp.concatenate(
        [jnp.where(use_first[0] != 0, a[...], b[...]) for a, b in zip(first, second)], 0
    )
    lefts[0, :, :tokens] = normed_early[...]
    lefts[0, :, tokens:] = normed_last[...]
    lefts[1, :, :tokens] = cot_early[...]
    lefts[1, :, tokens:] = cotangent.T
    grads[:tokens] = grads_early[...]
    hiddens[:tokens] = hidden_early[...]
    hiddens[tokens:] = hidden_last[...]
    waited(copies)
    hidden_grad = dot(cotangent, weights[:, down])
    grads[tokens:, :units] = (hidden_grad * slope[...]).astype(BF16)
    grads[tokens:, units:] = (hidden_grad * activated[...]).astype(BF16)
    for i, out in enumerate(outs):
        rows = slice(i * out.shape[0], (i + 1) * out.shape[0])
        out[:, : 2 * units] = dot(lefts[0, rows], grads[...]).astype(BF16)
        out[:, 2 * units :] = dot(lefts[1, rows], hiddens[...]).astype(BF16)


def mix_kernel(crossing, d, *refs):
    total = d[...].astype(F32) + total_of([r[...] for r in refs[:4]])
    rows = total.astype(BF16)
    if crossing:
        rows = dot(rows, refs[4][...]).astype(BF16)
    refs[-1][...] = rows


def add_kernel(*refs):
    total = total_of([r[...] for r in refs[:4]])
    outs = refs[4:]
    rows = total.shape[0] // len(outs)
    for i, out in enumerate(outs):
        out[...] = total[i * rows : (i + 1) * rows].astype(out.dtype)


def finish_kernel(*refs):
    total = total_of([r[...] for r in refs[:4]])
    refs[4][...] = total
    squares = jnp.sum(total * total, axis=0, keepdims=True)
    refs[5][...] = jnp.broadcast_to(jnp.sum(squares, axis=1, keepdims=True), refs[5].shape)


def near_pieces(pieces):
    return {by: from_plane(pieces[by], -by, False) for by in (1, 3)}


def far_piece(piece):
    return {2: from_plane(piece, -2, False)}


def add_pieces(own, got):
    share, wide = own.shape[0] // SIDE, own.shape[1]
    outs = [((share, wide), F32)] + [((share, wide), BF16)] * 3
    return run(add_kernel, [own, got[1], got[2], got[3]], outs, name="add")


def own_rows(sums):
    parts = [sums[0]] + peers(lambda by: from_plane(sums[by], -by, True))
    return run(finish_kernel, parts, [(sums[0].shape, F32), ((8, 128), F32)], name="finish")


def reduced_group(first_group, got, matrix):
    return run(
        functools.partial(mix_kernel, matrix is not None),
        [first_group] + got + ([] if matrix is None else [matrix]),
        [(first_group.shape, BF16)],
        name="mix",
    )[0]


def scattered(parts):
    return [parts[0]] + peers(lambda by: from_z(parts[by], -by))


def shared_groups(mine):
    return [mine] + peers(lambda by: from_z(mine, by))


def summed_everywhere(value):
    value = value + from_other_core(value)
    value = total_of([value] + peers(lambda by: from_plane(value, by, True)))
    value = total_of([value] + peers(lambda by: from_plane(value, by, False)))
    return total_of([value] + peers(lambda by: from_z(value, by)))[0, 0]


def per_device(
    saved_inputs,
    early_cotangents,
    final_cotangent,
    valid_counts,
    master,
    first_moment,
    second_moment,
):
    tokens, width = saved_inputs.shape[3:]
    units = master.shape[4]
    share = width // lax.axis_size("dp")
    section = lax.axis_index("pipe")
    place = lax.axis_index("dp")
    place_y, place_x = place // SIDE, place % SIDE
    place_z = lax.axis_index("tensor")
    group = tokens // SIDE
    wide = 3 * units
    on_first = (section == 0).astype(jnp.int32).reshape(1)
    on_second = 1 - on_first

    def as_stored(array):
        return array[0].transpose(0, 2, 1, 3)

    masters = as_stored(master)

    def shard_of(leg):
        return masters[:, :, leg, :].astype(BF16).reshape(share, wide)

    shard = shard_of(1)
    block = jnp.concatenate([shard] + peers(lambda by: from_plane(shard, by, True)), 0)
    lower_whole = lax.all_gather(shard_of(0), "dp", axis=0, tiled=True)
    upper = [block] + peers(lambda by: from_plane(block, by, False))
    saved_inputs, early_cotangents, final_cotangent = after(
        (saved_inputs, early_cotangents, final_cotangent), block
    )

    block = jnp.arange(width) // share
    outer, inner = block // SIDE, block % SIDE
    by_y = jnp.where(section == 0, outer, inner)
    by_x = jnp.where(section == 0, inner, outer)
    source_block = ((place_y + by_y) % SIDE) * SIDE + (place_x + by_x) % SIDE
    source_column = source_block * share + jnp.arange(width) % share
    mover = (jnp.arange(width)[:, None] == source_column[None, :]).astype(BF16)
    swapped_column = (inner * SIDE + outer) * share + jnp.arange(width) % share
    swap = (jnp.arange(width)[:, None] == swapped_column[None, :]).astype(BF16)
    turns = [(place_z + j) % SIDE for j in range(SIDE)]

    def turned(rows):
        return jnp.concatenate(
            [lax.dynamic_slice_in_dim(rows, turn * group, group, rows.ndim - 2) for turn in turns],
            rows.ndim - 2,
        )

    def moved(rows):
        return jnp.dot(turned(rows), mover, preferred_element_type=F32).astype(BF16)

    inputs = moved(saved_inputs[0])
    position = turned(lax.broadcasted_iota(jnp.int32, (tokens, 1), 0))
    early = jnp.where(position < valid_counts[0, 0], moved(early_cotangents[0]), 0)
    final = jnp.where(position < valid_counts[0, 1], moved(final_cotangent), 0)
    final_groups = [final[i * group : (i + 1) * group] for i in range(SIDE)]

    flop = 2 * tokens * width * units
    whole = [((width, wide), BF16)]
    half_outs = [
        ((width, tokens), BF16),
        ((tokens, units), BF16),
        ((tokens, units), F32),
        ((tokens, units), F32),
    ]
    group_outs = [((group, width), BF16)] * SIDE

    def far(arrays):
        return [(array, pltpu.HBM) for array in arrays]

    def fetched(columns):
        return [pltpu.VMEM((width, columns), BF16), pltpu.SemaphoreType.DMA((6,))]

    def early_parts(leg, leg_inputs, weights):
        one = len(weights) == 1
        return run(
            functools.partial(early_kernel, units),
            [leg_inputs, early[leg], *(weights if one else far(weights))],
            [
                ((width, tokens), BF16),
                ((width, tokens), BF16),
                ((tokens, units), BF16),
                ((tokens, 2 * units), BF16),
            ],
            [] if one else fetched(wide),
            5 * flop,
            "early",
        )

    def terms(use_first, first, second, early_half, half, weights):
        one = len(weights) == 1
        return run(
            functools.partial(terms_kernel, units),
            [
                (use_first, pltpu.SMEM),
                *first,
                *second,
                *early_half,
                *half,
                *(weights if one else far(weights)),
            ],
            [((width // SIDE, wide), BF16)] * SIDE,
            ([] if one else fetched(units))
            + [
                pltpu.VMEM((2, width, 2 * tokens), BF16),
                pltpu.VMEM((2 * tokens, 2 * units), BF16),
                pltpu.VMEM((2 * tokens, units), BF16),
            ],
            7 * flop,
            "terms",
        )

    upper = after(upper, (inputs, early, final, mover))
    outs = run(
        functools.partial(first_kernel, units),
        [inputs[1, 1], final, *far(upper)],
        [(*out, pltpu.HBM) for out in half_outs] + group_outs,
        fetched(wide)
        + [pltpu.VMEM(*out) for out in half_outs]
        + [pltpu.SemaphoreType.DMA((SIDE,))],
        5 * flop,
        "first",
    )
    upper_half, part3 = outs[:4], outs[4:]
    got = scattered(part3)
    early_one = early_parts(1, after(inputs[1, 0], part3[0]), upper)
    mine2 = reduced_group(after(final_groups[0], early_one), got, swap)
    cot2 = [across(mine2, by, 0) for by in range(SIDE)]
    part2 = run(
        functools.partial(far_chain_kernel, units),
        [
            (on_second, pltpu.SMEM),
            inputs[1, 1],
            *far(upper_half[2:]),
            *far(upper),
            *cot2,
        ],
        group_outs,
        fetched(wide) + [pltpu.VMEM(*out) for out in half_outs[2:]],
        3 * flop,
        "chain",
    )

    got = [across(part2[by], -by, 1) for by in range(SIDE)]
    lower_whole = after(lower_whole, part2[0])
    (lower_weights,) = run(
        order_kernel,
        far([mover.T, lower_whole]),
        whole,
        [pltpu.VMEM((width, width), BF16), *fetched(wide)],
        2 * width * width * wide,
        "order",
    )
    mine1 = reduced_group(after(mine2, lower_weights), got, None)
    cot1 = [across(mine1, by, 0) for by in range(SIDE)]
    lower_half = run(
        functools.partial(gate_kernel, units),
        [after(inputs[0, 1], mine1), lower_weights],
        half_outs,
        flops=2 * flop,
        name="gate",
    )
    part1 = run(
        functools.partial(chain_kernel, units),
        [
            (on_second, pltpu.SMEM),
            inputs[0, 1],
            lower_half[2],
            lower_half[3],
            lower_weights,
            *cot1,
        ],
        group_outs,
        flops=3 * flop,
        name="chain",
    )
    got = [across(part1[by], -by, 1) for by in range(SIDE)]
    early_one = after(early_one, part1[0])
    upper_terms = terms(on_first, final_groups, cot2, early_one, upper_half, upper)
    mine0 = reduced_group(after(mine1, upper_terms[0]), got, swap)
    cot0 = shared_groups(mine0)
    upper_got = near_pieces(after(upper_terms, mine0))
    early_zero = early_parts(0, after(inputs[0, 0], mine0), [lower_weights])
    upper_got |= far_piece(after(upper_terms[2], cot0))
    lower_terms = terms(on_second, cot1, cot0, early_zero, lower_half, [lower_weights])

    lower_got = near_pieces(lower_terms) | far_piece(lower_terms[2])
    upper_sums = add_pieces(after(upper_terms[0], lower_terms[0]), upper_got)
    upper_gradient, upper_squares = own_rows(upper_sums)
    lower_gradient, lower_squares = own_rows(add_pieces(lower_terms[0], lower_got))
    gradient = jnp.stack(
        [rows.reshape(share, 3, units) for rows in (lower_gradient, upper_gradient)], 2
    )

    total = summed_everywhere(lower_squares + upper_squares)
    param_count = lax.axis_size("pipe") * 6 * width * units * lax.axis_size("tensor")
    clip_factor = jnp.minimum(1.0, math.sqrt(param_count) / (jnp.sqrt(total) + 1e-06))
    scaled = gradient * clip_factor
    moment_one = 0.9 * as_stored(first_moment).astype(F32) + 0.1 * scaled
    moment_two = 0.95 * as_stored(second_moment).astype(F32) + 0.05 * scaled * scaled
    update = (
        moment_one / (1.0 - 0.9**STEP) / (jnp.sqrt(moment_two / (1.0 - 0.95**STEP)) + 1e-08)
        + 0.1 * masters
    )
    results = (masters - 0.001 * update, moment_one.astype(BF16), moment_two.astype(BF16))
    return tuple(result.transpose(0, 2, 1, 3)[None] for result in results)


def solution(mesh):
    in_specs = (
        P("pipe", None, None, "dp", None),
        P("pipe", None, "dp", None),
        P("dp", None),
        P("dp", None),
        P("pipe", "dp", None, None, "tensor"),
        P("pipe", "dp", None, None, "tensor"),
        P("pipe", "dp", None, None, "tensor"),
    )
    out_specs = (
        P("pipe", "dp", None, None, "tensor"),
        P("pipe", "dp", None, None, "tensor"),
        P("pipe", "dp", None, None, "tensor"),
    )
    return jax.shard_map(
        per_device, mesh=mesh, in_specs=in_specs, out_specs=out_specs, check_vma=False
    )
```

```python
import functools
import math

import jax
import jax.numpy as jnp
from jax import lax
from jax.experimental import pallas as pl
from jax.experimental.pallas import tpu as pltpu
from jax.sharding import PartitionSpec as P

STEP = 20
SIDE = 4
F32 = jnp.float32
BF16 = jnp.bfloat16
ORDER = (1, 3, 2)
VMEM_LIMIT = 20 * 1024 * 1024


def peers(fetch):
    got = {by: fetch(by) for by in ORDER}
    return [got[by] for by in (1, 2, 3)]


def from_plane(value, by, first):
    pairs = []
    for core in range(2):
        for y in range(SIDE):
            for x in range(SIDE):
                if (core == 0) == first:
                    source = (y, (x + by) % SIDE)
                else:
                    source = ((y + by) % SIDE, x)
                base = core * SIDE * SIDE
                pairs.append((base + source[0] * SIDE + source[1], base + y * SIDE + x))
    return lax.ppermute(value, ("pipe", "dp"), pairs)


def from_z(value, by):
    pairs = [((z + by) % SIDE, z) for z in range(SIDE)]
    return lax.ppermute(value, "tensor", pairs)


def across(value, by, source):
    pairs = [(source * SIDE + (z + by) % SIDE, (1 - source) * SIDE + z) for z in range(SIDE)]
    pairs += [((1 - source) * SIDE + z, source * SIDE + z) for z in range(SIDE)]
    return lax.ppermute(value, ("pipe", "tensor"), pairs)


def from_other_core(value):
    return lax.ppermute(value, "pipe", [(0, 1), (1, 0)])


def total_of(parts):
    total = parts[0].astype(F32)
    for part in parts[1:]:
        total = total + part.astype(F32)
    return total


def run(kernel, ins, outs, scratch=(), flops=0, name=None, limit=VMEM_LIMIT):
    arrays, specs = [], []
    for item in ins:
        array, space = item if isinstance(item, tuple) else (item, pltpu.VMEM)
        arrays.append(array)
        specs.append(pl.BlockSpec(memory_space=space))
    moved = sum(a.size * a.dtype.itemsize for a in arrays)
    moved += sum(math.prod(o[0]) * jnp.dtype(o[1]).itemsize for o in outs)
    return pl.pallas_call(
        kernel,
        out_shape=[jax.ShapeDtypeStruct(o[0], o[1]) for o in outs],
        in_specs=specs,
        out_specs=[pl.BlockSpec(memory_space=o[2] if o[2:] else pltpu.VMEM) for o in outs],
        scratch_shapes=list(scratch),
        compiler_params=pltpu.CompilerParams(vmem_limit_bytes=limit),
        cost_estimate=pl.CostEstimate(flops=flops, bytes_accessed=moved, transcendentals=0),
        name=name,
    )(*arrays)


def after(value, *others):
    return lax.optimization_barrier((value, others))[0]


def normalized(inputs):
    values = inputs.astype(F32)
    root_mean = jnp.sqrt(jnp.mean(values * values, axis=-1, keepdims=True) + 1e-06)
    return values / root_mean, root_mean


def dot(left, right):
    return jnp.dot(left, right, preferred_element_type=F32)


def gate_parts(normed, weights, units):
    both = dot(normed, weights[0][...])
    gate, up_rows = both[:, :units], both[:, units:]
    sigmoid_gate = jax.nn.sigmoid(gate)
    activated = gate * sigmoid_gate
    hidden = (activated * up_rows).astype(BF16)
    slope = up_rows * sigmoid_gate * (1.0 + gate * (1.0 - sigmoid_gate))
    return hidden, slope, activated


def both_grads(cotangent, slope, activated, weights, units):
    hidden_grad = dot(cotangent, weights[1][...])
    return jnp.concatenate(
        [(hidden_grad * slope).astype(BF16), (hidden_grad * activated).astype(BF16)], 1
    )


def store_branch(grads, inputs, weights, units, outs):
    branch = lax.dot_general(
        grads, weights[0][...], (((1,), (1,)), ((), ())), preferred_element_type=F32
    )
    unit_rows, root_mean = normalized(inputs)
    centered = branch - unit_rows * jnp.mean(branch * unit_rows, axis=-1, keepdims=True)
    rows = (centered / root_mean).astype(BF16)
    group = rows.shape[0] // SIDE
    for i, out in enumerate(outs):
        out[...] = rows[i * group : (i + 1) * group]


def started(copies):
    for copy in copies:
        copy.start()
    return copies


def waited(copies):
    for copy in copies:
        copy.wait()


def weight_copies(pieces, weights, sems):
    rows, columns = pieces[0].shape[0], weights.shape[1]
    first = pieces[0].shape[1] - columns
    return started(
        [
            pltpu.make_async_copy(
                piece.at[:, pl.ds(first, columns)], weights.at[pl.ds(i * rows, rows)], sems.at[i]
            )
            for i, piece in enumerate(pieces)
        ]
    )


def apart(weights, units):
    return weights.at[:, pl.ds(0, 2 * units)], weights.at[:, pl.ds(2 * units, units)]


def order_kernel(first, mover, whole, out, matrix, weights, sems):
    count = sems.shape[0] - 1
    columns = out.shape[1] // count
    copies = [pltpu.make_async_copy(mover, matrix, sems.at[0])]
    for i in range(count):
        source = whole.at[:, pl.ds(first + i * columns, columns)]
        target = weights.at[:, pl.ds(i * columns, columns)]
        copies.append(pltpu.make_async_copy(source, target, sems.at[i + 1]))
    started(copies)
    copies[0].wait()
    for i in range(count):
        copies[i + 1].wait()
        part = slice(i * columns, (i + 1) * columns)
        out[:, part] = dot(matrix[...], weights[:, part]).astype(BF16)


def gate_kernel(units, x, weights, *outs):
    normed = normalized(x[...])[0].astype(BF16)
    outs[0][...] = normed.T
    outs[1][...], outs[2][...], outs[3][...] = gate_parts(normed, (weights,), units)


def first_kernel(units, x, d, *refs):
    pieces, halves, outs = refs[:4], refs[4:8], refs[8:12]
    weights, sems, stages, out_sems = refs[12], refs[13], refs[14:18], refs[18]
    copies = weight_copies(pieces, weights, sems)
    weights = apart(weights, units)
    sends = [
        pltpu.make_async_copy(stage, half, out_sems.at[i])
        for i, (stage, half) in enumerate(zip(stages, halves))
    ]
    normed = normalized(x[...])[0].astype(BF16)
    stages[0][...] = normed.T
    sends[0].start()
    waited(copies)
    hidden, slope, activated = gate_parts(normed, weights, units)
    stages[1][...], stages[2][...], stages[3][...] = hidden, slope, activated
    started(sends[1:])
    grads = both_grads(d[...], slope, activated, weights, units)
    store_branch(grads, x[...], weights, units, outs)
    waited(sends)


def chain_kernel(units, active, x, slope, activated, ins, down, *refs):
    groups, outs = refs[:4], refs[4:]

    @pl.when(active[0] != 0)
    def _():
        cotangent = jnp.concatenate([g[...] for g in groups], 0)
        grads = both_grads(cotangent, slope[...], activated[...], (ins, down), units)
        store_branch(grads, x[...], (ins, down), units, outs)

    @pl.when(active[0] == 0)
    def _():
        for out in outs:
            out[...] = jnp.zeros(out.shape, out.dtype)


def far_chain_kernel(units, active, x, slope, activated, *refs):
    pieces, groups, outs = refs[:4], refs[4:8], refs[8:12]
    weights, sems, slope_here, activated_here = refs[12:]

    @pl.when(active[0] != 0)
    def _():
        copies = weight_copies(pieces, weights, sems)
        copies += started(
            [
                pltpu.make_async_copy(slope, slope_here, sems.at[4]),
                pltpu.make_async_copy(activated, activated_here, sems.at[5]),
            ]
        )
        cotangent = jnp.concatenate([g[...] for g in groups], 0)
        waited(copies)
        grads = both_grads(cotangent, slope_here[...], activated_here[...], apart(weights, units), units)
        store_branch(grads, x[...], apart(weights, units), units, outs)

    @pl.when(active[0] == 0)
    def _():
        for out in outs:
            out[...] = jnp.zeros(out.shape, out.dtype)


def early_kernel(units, x, d, *refs):
    if len(refs) > 6:
        pieces, outs, weights, sems = refs[:4], refs[4:8], refs[8], refs[9]
        copies, weights = weight_copies(pieces, weights, sems), apart(weights, units)
    else:
        weights, outs, copies = refs[:2], refs[2:], []
    normed = normalized(x[...])[0].astype(BF16)
    outs[0][...] = normed.T
    outs[1][...] = d[...].T
    waited(copies)
    hidden, slope, activated = gate_parts(normed, weights, units)
    outs[2][...] = hidden
    outs[3][...] = both_grads(d[...], slope, activated, weights, units)


def terms_kernel(units, use_first, *refs):
    first, second = refs[:4], refs[4:8]
    normed_early, cot_early, hidden_early, grads_early = refs[8:12]
    normed_last, hidden_last, slope, activated = refs[12:16]
    lefts, grads, hiddens = refs[-3:]
    if len(refs) > 24:
        pieces, outs, weights, sems = refs[16:20], refs[20:24], refs[24], refs[25]
        copies = weight_copies(pieces, weights, sems)
    else:
        weights, outs, copies = refs[16], refs[17:21], []
    tokens = normed_early.shape[1]
    cotangent = jnp.concatenate(
        [jnp.where(use_first[0] != 0, a[...], b[...]) for a, b in zip(first, second)], 0
    )
    lefts[0, :, :tokens] = normed_early[...]
    lefts[0, :, tokens:] = normed_last[...]
    lefts[1, :, :tokens] = cot_early[...]
    lefts[1, :, tokens:] = cotangent.T
    grads[:tokens] = grads_early[...]
    hiddens[:tokens] = hidden_early[...]
    hiddens[tokens:] = hidden_last[...]
    waited(copies)
    hidden_grad = dot(cotangent, weights[...])
    grads[tokens:, :units] = (hidden_grad * slope[...]).astype(BF16)
    grads[tokens:, units:] = (hidden_grad * activated[...]).astype(BF16)
    for i, out in enumerate(outs):
        rows = slice(i * out.shape[0], (i + 1) * out.shape[0])
        out[:, : 2 * units] = dot(lefts[0, rows], grads[...]).astype(BF16)
        out[:, 2 * units :] = dot(lefts[1, rows], hiddens[...]).astype(BF16)


def mix_kernel(crossing, d, *refs):
    total = d[...].astype(F32) + total_of([r[...] for r in refs[:4]])
    rows = total.astype(BF16)
    if crossing:
        rows = dot(rows, refs[4][...]).astype(BF16)
    refs[-1][...] = rows


def add_kernel(*refs):
    total = total_of([r[...] for r in refs[:4]])
    outs = refs[4:]
    rows = total.shape[0] // len(outs)
    for i, out in enumerate(outs):
        out[...] = total[i * rows : (i + 1) * rows].astype(out.dtype)


def finish_kernel(*refs):
    total = total_of([r[...] for r in refs[:4]])
    refs[4][...] = total
    squares = jnp.sum(total * total, axis=0, keepdims=True)
    refs[5][...] = jnp.broadcast_to(jnp.sum(squares, axis=1, keepdims=True), refs[5].shape)


def near_pieces(pieces):
    return {by: from_plane(pieces[by], -by, False) for by in (1, 3)}


def far_piece(piece):
    return {2: from_plane(piece, -2, False)}


def add_pieces(own, got):
    share, wide = own.shape[0] // SIDE, own.shape[1]
    outs = [((share, wide), F32)] + [((share, wide), BF16)] * 3
    return run(add_kernel, [own, got[1], got[2], got[3]], outs, name="add")


def own_rows(sums):
    parts = [sums[0]] + peers(lambda by: from_plane(sums[by], -by, True))
    return run(finish_kernel, parts, [(sums[0].shape, F32), ((8, 128), F32)], name="finish")


def reduced_group(first_group, got, matrix):
    return run(
        functools.partial(mix_kernel, matrix is not None),
        [first_group] + got + ([] if matrix is None else [matrix]),
        [(first_group.shape, BF16)],
        name="mix",
    )[0]


def scattered(parts):
    return [parts[0]] + peers(lambda by: from_z(parts[by], -by))


def shared_groups(mine):
    return [mine] + peers(lambda by: from_z(mine, by))


def summed_everywhere(value):
    value = value + from_other_core(value)
    value = total_of([value] + peers(lambda by: from_plane(value, by, True)))
    value = total_of([value] + peers(lambda by: from_plane(value, by, False)))
    return total_of([value] + peers(lambda by: from_z(value, by)))[0, 0]


def per_device(
    saved_inputs,
    early_cotangents,
    final_cotangent,
    valid_counts,
    master,
    first_moment,
    second_moment,
):
    tokens, width = saved_inputs.shape[3:]
    units = master.shape[4]
    share = width // lax.axis_size("dp")
    section = lax.axis_index("pipe")
    place = lax.axis_index("dp")
    place_y, place_x = place // SIDE, place % SIDE
    place_z = lax.axis_index("tensor")
    group = tokens // SIDE
    wide = 3 * units
    on_first = (section == 0).astype(jnp.int32).reshape(1)
    on_second = 1 - on_first

    def as_stored(array):
        return array[0].transpose(0, 2, 1, 3)

    masters = as_stored(master)

    def shard_of(leg):
        return masters[:, :, leg, :].astype(BF16).reshape(share, wide)

    shard = shard_of(1)
    block = jnp.concatenate([shard] + peers(lambda by: from_plane(shard, by, True)), 0)
    lower_whole = lax.all_gather(shard_of(0), "dp", axis=0, tiled=True)
    upper = [block] + peers(lambda by: from_plane(block, by, False))
    saved_inputs, early_cotangents, final_cotangent = after(
        (saved_inputs, early_cotangents, final_cotangent), block
    )

    block = jnp.arange(width) // share
    outer, inner = block // SIDE, block % SIDE
    by_y = jnp.where(section == 0, outer, inner)
    by_x = jnp.where(section == 0, inner, outer)
    source_block = ((place_y + by_y) % SIDE) * SIDE + (place_x + by_x) % SIDE
    source_column = source_block * share + jnp.arange(width) % share
    mover = (jnp.arange(width)[:, None] == source_column[None, :]).astype(BF16)
    swapped_column = (inner * SIDE + outer) * share + jnp.arange(width) % share
    swap = (jnp.arange(width)[:, None] == swapped_column[None, :]).astype(BF16)
    turns = [(place_z + j) % SIDE for j in range(SIDE)]

    def turned(rows):
        return jnp.concatenate(
            [lax.dynamic_slice_in_dim(rows, turn * group, group, rows.ndim - 2) for turn in turns],
            rows.ndim - 2,
        )

    def moved(rows):
        return jnp.dot(turned(rows), mover, preferred_element_type=F32).astype(BF16)

    inputs = moved(saved_inputs[0])
    position = turned(lax.broadcasted_iota(jnp.int32, (tokens, 1), 0))
    early = jnp.where(position < valid_counts[0, 0], moved(early_cotangents[0]), 0)
    final = jnp.where(position < valid_counts[0, 1], moved(final_cotangent), 0)
    final_groups = [final[i * group : (i + 1) * group] for i in range(SIDE)]

    flop = 2 * tokens * width * units
    half_outs = [
        ((width, tokens), BF16),
        ((tokens, units), BF16),
        ((tokens, units), F32),
        ((tokens, units), F32),
    ]
    group_outs = [((group, width), BF16)] * SIDE

    def far(arrays):
        return [(array, pltpu.HBM) for array in arrays]

    def fetched(columns):
        return [pltpu.VMEM((width, columns), BF16), pltpu.SemaphoreType.DMA((6,))]

    def early_parts(leg, leg_inputs, weights):
        one = len(weights) < 4
        return run(
            functools.partial(early_kernel, units),
            [leg_inputs, early[leg], *(weights if one else far(weights))],
            [
                ((width, tokens), BF16),
                ((width, tokens), BF16),
                ((tokens, units), BF16),
                ((tokens, 2 * units), BF16),
            ],
            [] if one else fetched(wide),
            5 * flop,
            "early",
        )

    def terms(use_first, first, second, early_half, half, weights):
        one = len(weights) < 4
        return run(
            functools.partial(terms_kernel, units),
            [
                (use_first, pltpu.SMEM),
                *first,
                *second,
                *early_half,
                *half,
                *(weights if one else far(weights)),
            ],
            [((width // SIDE, wide), BF16)] * SIDE,
            ([] if one else fetched(units))
            + [
                pltpu.VMEM((2, width, 2 * tokens), BF16),
                pltpu.VMEM((2 * tokens, 2 * units), BF16),
                pltpu.VMEM((2 * tokens, units), BF16),
            ],
            7 * flop,
            "terms",
        )

    upper = after(upper, (inputs, early, final, mover))
    outs = run(
        functools.partial(first_kernel, units),
        [inputs[1, 1], final, *far(upper)],
        [(*out, pltpu.HBM) for out in half_outs] + group_outs,
        fetched(wide)
        + [pltpu.VMEM(*out) for out in half_outs]
        + [pltpu.SemaphoreType.DMA((SIDE,))],
        5 * flop,
        "first",
    )
    upper_half, part3 = outs[:4], outs[4:]
    got = scattered(part3)
    early_one = early_parts(1, after(inputs[1, 0], part3[0]), upper)
    mine2 = reduced_group(after(final_groups[0], early_one), got, swap)
    cot2 = [across(mine2, by, 0) for by in range(SIDE)]
    part2 = run(
        functools.partial(far_chain_kernel, units),
        [
            (on_second, pltpu.SMEM),
            inputs[1, 1],
            *far(upper_half[2:]),
            *far(upper),
            *cot2,
        ],
        group_outs,
        fetched(wide) + [pltpu.VMEM(*out) for out in half_outs[2:]],
        3 * flop,
        "chain",
    )

    got = [across(part2[by], -by, 1) for by in range(SIDE)]

    def ordered(columns, count, *others):
        first, last = columns
        return run(
            functools.partial(order_kernel, first),
            far([mover.T, after(lower_whole, *others)]),
            [((width, last - first), BF16)],
            [
                pltpu.VMEM((width, width), BF16),
                pltpu.VMEM((width, last - first), BF16),
                pltpu.SemaphoreType.DMA((count + 1,)),
            ],
            2 * width * width * (last - first),
            "order",
        )[0]

    lower_ins = ordered((0, 2 * units), 2, part2[0])
    mine1 = reduced_group(after(mine2, lower_ins), got, None)
    cot1 = [across(mine1, by, 0) for by in range(SIDE)]
    lower_half = run(
        functools.partial(gate_kernel, units),
        [after(inputs[0, 1], mine1), lower_ins],
        half_outs,
        flops=2 * flop,
        name="gate",
    )
    lower_down = ordered((2 * units, 3 * units), 1, mine1)
    part1 = run(
        functools.partial(chain_kernel, units),
        [
            (on_second, pltpu.SMEM),
            inputs[0, 1],
            lower_half[2],
            lower_half[3],
            lower_ins,
            lower_down,
            *cot1,
        ],
        group_outs,
        flops=3 * flop,
        name="chain",
    )
    got = [across(part1[by], -by, 1) for by in range(SIDE)]
    early_one = after(early_one, part1[0])
    upper_terms = terms(on_first, final_groups, cot2, early_one, upper_half, upper)
    mine0 = reduced_group(after(mine1, upper_terms[0]), got, swap)
    cot0 = shared_groups(mine0)
    upper_got = near_pieces(after(upper_terms, mine0))
    early_zero = early_parts(0, after(inputs[0, 0], mine0), [lower_ins, lower_down])
    upper_got |= far_piece(after(upper_terms[2], cot0))
    early_zero = after(early_zero, [upper_got[by] for by in (1, 3)])
    lower_terms = terms(on_second, cot1, cot0, early_zero, lower_half, [lower_down])

    lower_got = near_pieces(lower_terms) | far_piece(lower_terms[2])
    upper_sums = add_pieces(after(upper_terms[0], lower_terms[0]), upper_got)
    upper_gradient, upper_squares = own_rows(upper_sums)
    lower_gradient, lower_squares = own_rows(add_pieces(lower_terms[0], lower_got))
    gradient = jnp.stack(
        [rows.reshape(share, 3, units) for rows in (lower_gradient, upper_gradient)], 2
    )

    total = summed_everywhere(lower_squares + upper_squares)
    param_count = lax.axis_size("pipe") * 6 * width * units * lax.axis_size("tensor")
    clip_factor = jnp.minimum(1.0, math.sqrt(param_count) / (jnp.sqrt(total) + 1e-06))
    scaled = gradient * clip_factor
    moment_one = 0.9 * as_stored(first_moment).astype(F32) + 0.1 * scaled
    moment_two = 0.95 * as_stored(second_moment).astype(F32) + 0.05 * scaled * scaled
    update = (
        moment_one / (1.0 - 0.9**STEP) / (jnp.sqrt(moment_two / (1.0 - 0.95**STEP)) + 1e-08)
        + 0.1 * masters
    )
    results = (masters - 0.001 * update, moment_one.astype(BF16), moment_two.astype(BF16))
    return tuple(result.transpose(0, 2, 1, 3)[None] for result in results)


def solution(mesh):
    in_specs = (
        P("pipe", None, None, "dp", None),
        P("pipe", None, "dp", None),
        P("dp", None),
        P("dp", None),
        P("pipe", "dp", None, None, "tensor"),
        P("pipe", "dp", None, None, "tensor"),
        P("pipe", "dp", None, None, "tensor"),
    )
    out_specs = (
        P("pipe", "dp", None, None, "tensor"),
        P("pipe", "dp", None, None, "tensor"),
        P("pipe", "dp", None, None, "tensor"),
    )
    return jax.shard_map(
        per_device, mesh=mesh, in_specs=in_specs, out_specs=out_specs, check_vma=False
    )
```

```python
import functools
import math

import jax
import jax.numpy as jnp
from jax import lax
from jax.experimental import pallas as pl
from jax.experimental.pallas import tpu as pltpu
from jax.sharding import PartitionSpec as P

STEP = 20
SIDE = 4
F32 = jnp.float32
BF16 = jnp.bfloat16
ORDER = (1, 3, 2)
VMEM_LIMIT = 20 * 1024 * 1024


def peers(fetch):
    got = {by: fetch(by) for by in ORDER}
    return [got[by] for by in (1, 2, 3)]


def from_plane(value, by, first):
    pairs = []
    for core in range(2):
        for y in range(SIDE):
            for x in range(SIDE):
                if (core == 0) == first:
                    source = (y, (x + by) % SIDE)
                else:
                    source = ((y + by) % SIDE, x)
                base = core * SIDE * SIDE
                pairs.append((base + source[0] * SIDE + source[1], base + y * SIDE + x))
    return lax.ppermute(value, ("pipe", "dp"), pairs)


def from_z(value, by):
    pairs = [((z + by) % SIDE, z) for z in range(SIDE)]
    return lax.ppermute(value, "tensor", pairs)


def across(value, by, source):
    pairs = [(source * SIDE + (z + by) % SIDE, (1 - source) * SIDE + z) for z in range(SIDE)]
    pairs += [((1 - source) * SIDE + z, source * SIDE + z) for z in range(SIDE)]
    return lax.ppermute(value, ("pipe", "tensor"), pairs)


def from_other_core(value):
    return lax.ppermute(value, "pipe", [(0, 1), (1, 0)])


def total_of(parts):
    total = parts[0].astype(F32)
    for part in parts[1:]:
        total = total + part.astype(F32)
    return total


def run(kernel, ins, outs, scratch=(), flops=0, name=None, limit=VMEM_LIMIT):
    arrays, specs = [], []
    for item in ins:
        array, space = item if isinstance(item, tuple) else (item, pltpu.VMEM)
        arrays.append(array)
        specs.append(pl.BlockSpec(memory_space=space))
    moved = sum(a.size * a.dtype.itemsize for a in arrays)
    moved += sum(math.prod(o[0]) * jnp.dtype(o[1]).itemsize for o in outs)
    return pl.pallas_call(
        kernel,
        out_shape=[jax.ShapeDtypeStruct(o[0], o[1]) for o in outs],
        in_specs=specs,
        out_specs=[pl.BlockSpec(memory_space=o[2] if o[2:] else pltpu.VMEM) for o in outs],
        scratch_shapes=list(scratch),
        compiler_params=pltpu.CompilerParams(vmem_limit_bytes=limit),
        cost_estimate=pl.CostEstimate(flops=flops, bytes_accessed=moved, transcendentals=0),
        name=name,
    )(*arrays)


def after(value, *others):
    return lax.optimization_barrier((value, others))[0]


def normalized(inputs):
    values = inputs.astype(F32)
    root_mean = jnp.sqrt(jnp.mean(values * values, axis=-1, keepdims=True) + 1e-06)
    return values / root_mean, root_mean


def dot(left, right):
    return jnp.dot(left, right, preferred_element_type=F32)


def gate_parts(normed, weights, units):
    both = dot(normed, weights[0][...])
    gate, up_rows = both[:, :units], both[:, units:]
    sigmoid_gate = jax.nn.sigmoid(gate)
    activated = gate * sigmoid_gate
    hidden = (activated * up_rows).astype(BF16)
    slope = up_rows * sigmoid_gate * (1.0 + gate * (1.0 - sigmoid_gate))
    return hidden, slope, activated


def both_grads(cotangent, slope, activated, weights, units):
    hidden_grad = dot(cotangent, weights[1][...])
    return jnp.concatenate(
        [(hidden_grad * slope).astype(BF16), (hidden_grad * activated).astype(BF16)], 1
    )


def store_branch(grads, inputs, weights, units, outs):
    branch = lax.dot_general(
        grads, weights[0][...], (((1,), (1,)), ((), ())), preferred_element_type=F32
    )
    unit_rows, root_mean = normalized(inputs)
    centered = branch - unit_rows * jnp.mean(branch * unit_rows, axis=-1, keepdims=True)
    rows = (centered / root_mean).astype(BF16)
    group = rows.shape[0] // SIDE
    for i, out in enumerate(outs):
        out[...] = rows[i * group : (i + 1) * group]


def started(copies):
    for copy in copies:
        copy.start()
    return copies


def waited(copies):
    for copy in copies:
        copy.wait()


def weight_copies(pieces, weights, sems):
    rows, columns = pieces[0].shape[0], weights.shape[1]
    first = pieces[0].shape[1] - columns
    return started(
        [
            pltpu.make_async_copy(
                piece.at[:, pl.ds(first, columns)], weights.at[pl.ds(i * rows, rows)], sems.at[i]
            )
            for i, piece in enumerate(pieces)
        ]
    )


def apart(weights, units):
    return weights.at[:, pl.ds(0, 2 * units)], weights.at[:, pl.ds(2 * units, units)]


def order_kernel(first, mover, whole, out, matrix, weights, sems):
    count = sems.shape[0] - 1
    columns = out.shape[1] // count
    copies = [pltpu.make_async_copy(mover, matrix, sems.at[0])]
    for i in range(count):
        source = whole.at[:, pl.ds(first + i * columns, columns)]
        target = weights.at[:, pl.ds(i * columns, columns)]
        copies.append(pltpu.make_async_copy(source, target, sems.at[i + 1]))
    started(copies)
    copies[0].wait()
    for i in range(count):
        copies[i + 1].wait()
        part = slice(i * columns, (i + 1) * columns)
        out[:, part] = dot(matrix[...], weights[:, part]).astype(BF16)


def gate_kernel(units, x, weights, *outs):
    normed = normalized(x[...])[0].astype(BF16)
    outs[0][...] = normed.T
    outs[1][...], outs[2][...], outs[3][...] = gate_parts(normed, (weights,), units)


def first_kernel(units, x, d, *refs):
    pieces, halves, outs = refs[:4], refs[4:8], refs[8:12]
    weights, sems, stages, out_sems = refs[12], refs[13], refs[14:18], refs[18]
    copies = weight_copies(pieces, weights, sems)
    weights = apart(weights, units)
    sends = [
        pltpu.make_async_copy(stage, half, out_sems.at[i])
        for i, (stage, half) in enumerate(zip(stages, halves))
    ]
    normed = normalized(x[...])[0].astype(BF16)
    stages[0][...] = normed.T
    sends[0].start()
    waited(copies)
    hidden, slope, activated = gate_parts(normed, weights, units)
    stages[1][...], stages[2][...], stages[3][...] = hidden, slope, activated
    started(sends[1:])
    grads = both_grads(d[...], slope, activated, weights, units)
    store_branch(grads, x[...], weights, units, outs)
    waited(sends)


def chain_kernel(units, active, x, slope, activated, ins, down, *refs):
    groups, outs = refs[:4], refs[4:]

    @pl.when(active[0] != 0)
    def _():
        cotangent = jnp.concatenate([g[...] for g in groups], 0)
        grads = both_grads(cotangent, slope[...], activated[...], (ins, down), units)
        store_branch(grads, x[...], (ins, down), units, outs)

    @pl.when(active[0] == 0)
    def _():
        for out in outs:
            out[...] = jnp.zeros(out.shape, out.dtype)


def far_chain_kernel(units, active, x, slope, activated, *refs):
    pieces, groups, outs = refs[:4], refs[4:8], refs[8:12]
    weights, sems, slope_here, activated_here = refs[12:]

    @pl.when(active[0] != 0)
    def _():
        copies = weight_copies(pieces, weights, sems)
        copies += started(
            [
                pltpu.make_async_copy(slope, slope_here, sems.at[4]),
                pltpu.make_async_copy(activated, activated_here, sems.at[5]),
            ]
        )
        cotangent = jnp.concatenate([g[...] for g in groups], 0)
        waited(copies)
        grads = both_grads(cotangent, slope_here[...], activated_here[...], apart(weights, units), units)
        store_branch(grads, x[...], apart(weights, units), units, outs)

    @pl.when(active[0] == 0)
    def _():
        for out in outs:
            out[...] = jnp.zeros(out.shape, out.dtype)


def early_kernel(units, x, d, *refs):
    if len(refs) > 6:
        pieces, outs, weights, sems = refs[:4], refs[4:8], refs[8], refs[9]
        copies, weights = weight_copies(pieces, weights, sems), apart(weights, units)
    else:
        weights, outs, copies = refs[:2], refs[2:], []
    normed = normalized(x[...])[0].astype(BF16)
    outs[0][...] = normed.T
    outs[1][...] = d[...].T
    waited(copies)
    hidden, slope, activated = gate_parts(normed, weights, units)
    outs[2][...] = hidden
    outs[3][...] = both_grads(d[...], slope, activated, weights, units)


def terms_kernel(units, use_first, *refs):
    first, second = refs[:4], refs[4:8]
    normed_early, cot_early, hidden_early, grads_early = refs[8:12]
    normed_last, hidden_last, slope, activated = refs[12:16]
    lefts, grads, hiddens = refs[-3:]
    if len(refs) > 24:
        pieces, outs, weights, sems = refs[16:20], refs[20:24], refs[24], refs[25]
        copies = weight_copies(pieces, weights, sems)
    else:
        weights, outs, copies = refs[16], refs[17:21], []
    tokens = normed_early.shape[1]
    cotangent = jnp.concatenate(
        [jnp.where(use_first[0] != 0, a[...], b[...]) for a, b in zip(first, second)], 0
    )
    lefts[0, :, :tokens] = normed_early[...]
    lefts[0, :, tokens:] = normed_last[...]
    lefts[1, :, :tokens] = cot_early[...]
    lefts[1, :, tokens:] = cotangent.T
    grads[:tokens] = grads_early[...]
    hiddens[:tokens] = hidden_early[...]
    hiddens[tokens:] = hidden_last[...]
    waited(copies)
    hidden_grad = dot(cotangent, weights[...])
    grads[tokens:, :units] = (hidden_grad * slope[...]).astype(BF16)
    grads[tokens:, units:] = (hidden_grad * activated[...]).astype(BF16)
    for i, out in enumerate(outs):
        rows = slice(i * out.shape[0], (i + 1) * out.shape[0])
        out[:, : 2 * units] = dot(lefts[0, rows], grads[...]).astype(BF16)
        out[:, 2 * units :] = dot(lefts[1, rows], hiddens[...]).astype(BF16)


def mix_kernel(crossing, d, *refs):
    total = d[...].astype(F32) + total_of([r[...] for r in refs[:4]])
    rows = total.astype(BF16)
    if crossing:
        rows = dot(rows, refs[4][...]).astype(BF16)
    refs[-1][...] = rows


def add_kernel(*refs):
    total = total_of([r[...] for r in refs[:4]])
    outs = refs[4:]
    rows = total.shape[0] // len(outs)
    for i, out in enumerate(outs):
        out[...] = total[i * rows : (i + 1) * rows].astype(out.dtype)


def finish_kernel(*refs):
    total = total_of([r[...] for r in refs[:4]])
    refs[4][...] = total
    squares = jnp.sum(total * total, axis=0, keepdims=True)
    refs[5][...] = jnp.broadcast_to(jnp.sum(squares, axis=1, keepdims=True), refs[5].shape)


def near_pieces(pieces):
    return {by: from_plane(pieces[by], -by, False) for by in (1, 3)}


def far_piece(piece):
    return {2: from_plane(piece, -2, False)}


def add_pieces(own, got):
    share, wide = own.shape[0] // SIDE, own.shape[1]
    outs = [((share, wide), F32)] + [((share, wide), BF16)] * 3
    return run(add_kernel, [own, got[1], got[2], got[3]], outs, name="add")


def own_rows(sums):
    parts = [sums[0]] + peers(lambda by: from_plane(sums[by], -by, True))
    return run(finish_kernel, parts, [(sums[0].shape, F32), ((8, 128), F32)], name="finish")


def reduced_group(first_group, got, matrix):
    return run(
        functools.partial(mix_kernel, matrix is not None),
        [first_group] + got + ([] if matrix is None else [matrix]),
        [(first_group.shape, BF16)],
        name="mix",
    )[0]


def scattered(parts):
    return [parts[0]] + peers(lambda by: from_z(parts[by], -by))


def shared_groups(mine):
    return [mine] + peers(lambda by: from_z(mine, by))


def summed_everywhere(value):
    value = value + from_other_core(value)
    for stride in (1, SIDE):

        def along(by):
            pairs = []
            for i in range(SIDE * SIDE):
                at = i // stride % SIDE
                pairs.append((i + ((at + by) % SIDE - at) * stride, i))
            return lax.ppermute(value, "dp", pairs)

        value = total_of([value] + peers(along))
    return total_of([value] + peers(lambda by: from_z(value, by)))[0, 0]


def per_device(
    saved_inputs,
    early_cotangents,
    final_cotangent,
    valid_counts,
    master,
    first_moment,
    second_moment,
):
    tokens, width = saved_inputs.shape[3:]
    units = master.shape[4]
    share = width // lax.axis_size("dp")
    section = lax.axis_index("pipe")
    place = lax.axis_index("dp")
    place_y, place_x = place // SIDE, place % SIDE
    place_z = lax.axis_index("tensor")
    group = tokens // SIDE
    wide = 3 * units
    on_first = (section == 0).astype(jnp.int32).reshape(1)
    on_second = 1 - on_first

    def as_stored(array):
        return array[0].transpose(0, 2, 1, 3)

    masters = as_stored(master)

    def shard_of(leg):
        return masters[:, :, leg, :].astype(BF16).reshape(share, wide)

    shard = shard_of(1)
    block = jnp.concatenate([shard] + peers(lambda by: from_plane(shard, by, True)), 0)
    lower_whole = lax.all_gather(shard_of(0), "dp", axis=0, tiled=True)
    upper = [block] + peers(lambda by: from_plane(block, by, False))
    saved_inputs, early_cotangents, final_cotangent = after(
        (saved_inputs, early_cotangents, final_cotangent), block
    )

    block = jnp.arange(width) // share
    outer, inner = block // SIDE, block % SIDE
    by_y = jnp.where(section == 0, outer, inner)
    by_x = jnp.where(section == 0, inner, outer)
    source_block = ((place_y + by_y) % SIDE) * SIDE + (place_x + by_x) % SIDE
    source_column = source_block * share + jnp.arange(width) % share
    mover = (jnp.arange(width)[:, None] == source_column[None, :]).astype(BF16)
    swapped_column = (inner * SIDE + outer) * share + jnp.arange(width) % share
    swap = (jnp.arange(width)[:, None] == swapped_column[None, :]).astype(BF16)
    turns = [(place_z + j) % SIDE for j in range(SIDE)]

    def turned(rows):
        return jnp.concatenate(
            [lax.dynamic_slice_in_dim(rows, turn * group, group, rows.ndim - 2) for turn in turns],
            rows.ndim - 2,
        )

    def moved(rows):
        return jnp.dot(turned(rows), mover, preferred_element_type=F32).astype(BF16)

    inputs = moved(saved_inputs[0])
    position = turned(lax.broadcasted_iota(jnp.int32, (tokens, 1), 0))
    early = jnp.where(position < valid_counts[0, 0], moved(early_cotangents[0]), 0)
    final = jnp.where(position < valid_counts[0, 1], moved(final_cotangent), 0)
    final_groups = [final[i * group : (i + 1) * group] for i in range(SIDE)]

    flop = 2 * tokens * width * units
    half_outs = [
        ((width, tokens), BF16),
        ((tokens, units), BF16),
        ((tokens, units), F32),
        ((tokens, units), F32),
    ]
    group_outs = [((group, width), BF16)] * SIDE

    def far(arrays):
        return [(array, pltpu.HBM) for array in arrays]

    def fetched(columns):
        return [pltpu.VMEM((width, columns), BF16), pltpu.SemaphoreType.DMA((6,))]

    def early_parts(leg, leg_inputs, weights):
        one = len(weights) < 4
        return run(
            functools.partial(early_kernel, units),
            [leg_inputs, early[leg], *(weights if one else far(weights))],
            [
                ((width, tokens), BF16),
                ((width, tokens), BF16),
                ((tokens, units), BF16),
                ((tokens, 2 * units), BF16),
            ],
            [] if one else fetched(wide),
            5 * flop,
            "early",
        )

    def terms(use_first, first, second, early_half, half, weights):
        one = len(weights) < 4
        return run(
            functools.partial(terms_kernel, units),
            [
                (use_first, pltpu.SMEM),
                *first,
                *second,
                *early_half,
                *half,
                *(weights if one else far(weights)),
            ],
            [((width // SIDE, wide), BF16)] * SIDE,
            ([] if one else fetched(units))
            + [
                pltpu.VMEM((2, width, 2 * tokens), BF16),
                pltpu.VMEM((2 * tokens, 2 * units), BF16),
                pltpu.VMEM((2 * tokens, units), BF16),
            ],
            7 * flop,
            "terms",
        )

    upper = after(upper, (inputs, early, final, mover))
    outs = run(
        functools.partial(first_kernel, units),
        [inputs[1, 1], final, *far(upper)],
        [(*out, pltpu.HBM) for out in half_outs] + group_outs,
        fetched(wide)
        + [pltpu.VMEM(*out) for out in half_outs]
        + [pltpu.SemaphoreType.DMA((SIDE,))],
        5 * flop,
        "first",
    )
    upper_half, part3 = outs[:4], outs[4:]
    got = scattered(part3)
    early_one = early_parts(1, after(inputs[1, 0], part3[0]), upper)
    mine2 = reduced_group(after(final_groups[0], early_one), got, swap)
    cot2 = [across(mine2, by, 0) for by in range(SIDE)]
    part2 = run(
        functools.partial(far_chain_kernel, units),
        [
            (on_second, pltpu.SMEM),
            inputs[1, 1],
            *far(upper_half[2:]),
            *far(upper),
            *cot2,
        ],
        group_outs,
        fetched(wide) + [pltpu.VMEM(*out) for out in half_outs[2:]],
        3 * flop,
        "chain",
    )

    got = [across(part2[by], -by, 1) for by in range(SIDE)]

    def ordered(columns, count, *others):
        first, last = columns
        return run(
            functools.partial(order_kernel, first),
            far([mover.T, after(lower_whole, *others)]),
            [((width, last - first), BF16)],
            [
                pltpu.VMEM((width, width), BF16),
                pltpu.VMEM((width, last - first), BF16),
                pltpu.SemaphoreType.DMA((count + 1,)),
            ],
            2 * width * width * (last - first),
            "order",
        )[0]

    lower_ins = ordered((0, 2 * units), 2, part2[0])
    mine1 = reduced_group(after(mine2, lower_ins), got, None)
    cot1 = [across(mine1, by, 0) for by in range(SIDE)]
    lower_half = run(
        functools.partial(gate_kernel, units),
        [after(inputs[0, 1], mine1), lower_ins],
        half_outs,
        flops=2 * flop,
        name="gate",
    )
    lower_down = ordered((2 * units, 3 * units), 1, mine1)
    part1 = run(
        functools.partial(chain_kernel, units),
        [
            (on_second, pltpu.SMEM),
            inputs[0, 1],
            lower_half[2],
            lower_half[3],
            lower_ins,
            lower_down,
            *cot1,
        ],
        group_outs,
        flops=3 * flop,
        name="chain",
    )
    got = [across(part1[by], -by, 1) for by in range(SIDE)]
    early_one = after(early_one, part1[0])
    upper_terms = terms(on_first, final_groups, cot2, early_one, upper_half, upper)
    mine0 = reduced_group(after(mine1, upper_terms[0]), got, swap)
    cot0 = shared_groups(mine0)
    upper_got = near_pieces(after(upper_terms, mine0))
    early_zero = early_parts(0, after(inputs[0, 0], mine0), [lower_ins, lower_down])
    upper_got |= far_piece(after(upper_terms[2], cot0))
    early_zero = after(early_zero, [upper_got[by] for by in (1, 3)])
    lower_terms = terms(on_second, cot1, cot0, early_zero, lower_half, [lower_down])

    lower_got = near_pieces(lower_terms) | far_piece(lower_terms[2])
    upper_sums = add_pieces(after(upper_terms[0], lower_terms[0]), upper_got)
    upper_gradient, upper_squares = own_rows(upper_sums)
    lower_gradient, lower_squares = own_rows(add_pieces(lower_terms[0], lower_got))
    gradient = jnp.stack(
        [rows.reshape(share, 3, units) for rows in (lower_gradient, upper_gradient)], 2
    )

    total = summed_everywhere(lower_squares + upper_squares)
    param_count = lax.axis_size("pipe") * 6 * width * units * lax.axis_size("tensor")
    clip_factor = jnp.minimum(1.0, math.sqrt(param_count) / (jnp.sqrt(total) + 1e-06))
    scaled = gradient * clip_factor
    moment_one = 0.9 * as_stored(first_moment).astype(F32) + 0.1 * scaled
    moment_two = 0.95 * as_stored(second_moment).astype(F32) + 0.05 * scaled * scaled
    update = (
        moment_one / (1.0 - 0.9**STEP) / (jnp.sqrt(moment_two / (1.0 - 0.95**STEP)) + 1e-08)
        + 0.1 * masters
    )
    results = (masters - 0.001 * update, moment_one.astype(BF16), moment_two.astype(BF16))
    return tuple(result.transpose(0, 2, 1, 3)[None] for result in results)


def solution(mesh):
    in_specs = (
        P("pipe", None, None, "dp", None),
        P("pipe", None, "dp", None),
        P("dp", None),
        P("dp", None),
        P("pipe", "dp", None, None, "tensor"),
        P("pipe", "dp", None, None, "tensor"),
        P("pipe", "dp", None, None, "tensor"),
    )
    out_specs = (
        P("pipe", "dp", None, None, "tensor"),
        P("pipe", "dp", None, None, "tensor"),
        P("pipe", "dp", None, None, "tensor"),
    )
    return jax.shard_map(
        per_device, mesh=mesh, in_specs=in_specs, out_specs=out_specs, check_vma=False
    )
```

```python
import functools
import math

import jax
import jax.numpy as jnp
from jax import lax
from jax.experimental import pallas as pl
from jax.experimental.pallas import tpu as pltpu
from jax.sharding import PartitionSpec as P

STEP = 20
SIDE = 4
F32 = jnp.float32
BF16 = jnp.bfloat16
ORDER = (1, 3, 2)
VMEM_LIMIT = 20 * 1024 * 1024


def peers(fetch):
    got = {by: fetch(by) for by in ORDER}
    return [got[by] for by in (1, 2, 3)]


def from_plane(value, by, first):
    pairs = []
    for core in range(2):
        for y in range(SIDE):
            for x in range(SIDE):
                if (core == 0) == first:
                    source = (y, (x + by) % SIDE)
                else:
                    source = ((y + by) % SIDE, x)
                base = core * SIDE * SIDE
                pairs.append((base + source[0] * SIDE + source[1], base + y * SIDE + x))
    return lax.ppermute(value, ("pipe", "dp"), pairs)


def from_z(value, by):
    pairs = [((z + by) % SIDE, z) for z in range(SIDE)]
    return lax.ppermute(value, "tensor", pairs)


def across(value, by, source):
    pairs = [(source * SIDE + (z + by) % SIDE, (1 - source) * SIDE + z) for z in range(SIDE)]
    pairs += [((1 - source) * SIDE + z, source * SIDE + z) for z in range(SIDE)]
    return lax.ppermute(value, ("pipe", "tensor"), pairs)


def from_other_core(value):
    return lax.ppermute(value, "pipe", [(0, 1), (1, 0)])


def total_of(parts):
    total = parts[0].astype(F32)
    for part in parts[1:]:
        total = total + part.astype(F32)
    return total


def run(kernel, ins, outs, scratch=(), flops=0, name=None, limit=VMEM_LIMIT):
    arrays, specs = [], []
    for item in ins:
        array, space = item if isinstance(item, tuple) else (item, pltpu.VMEM)
        arrays.append(array)
        specs.append(pl.BlockSpec(memory_space=space))
    moved = sum(a.size * a.dtype.itemsize for a in arrays)
    moved += sum(math.prod(o[0]) * jnp.dtype(o[1]).itemsize for o in outs)
    return pl.pallas_call(
        kernel,
        out_shape=[jax.ShapeDtypeStruct(o[0], o[1]) for o in outs],
        in_specs=specs,
        out_specs=[pl.BlockSpec(memory_space=o[2] if o[2:] else pltpu.VMEM) for o in outs],
        scratch_shapes=list(scratch),
        compiler_params=pltpu.CompilerParams(vmem_limit_bytes=limit),
        cost_estimate=pl.CostEstimate(flops=flops, bytes_accessed=moved, transcendentals=0),
        name=name,
    )(*arrays)


def after(value, *others):
    return lax.optimization_barrier((value, others))[0]


def normalized(inputs):
    values = inputs.astype(F32)
    root_mean = jnp.sqrt(jnp.mean(values * values, axis=-1, keepdims=True) + 1e-06)
    return values / root_mean, root_mean


def dot(left, right):
    return jnp.dot(left, right, preferred_element_type=F32)


def gate_parts(normed, weights, units):
    both = dot(normed, weights[0][...])
    gate, up_rows = both[:, :units], both[:, units:]
    sigmoid_gate = jax.nn.sigmoid(gate)
    activated = gate * sigmoid_gate
    hidden = (activated * up_rows).astype(BF16)
    slope = up_rows * sigmoid_gate * (1.0 + gate * (1.0 - sigmoid_gate))
    return hidden, slope, activated


def both_grads(cotangent, slope, activated, weights, units):
    hidden_grad = dot(cotangent, weights[1][...])
    return jnp.concatenate(
        [(hidden_grad * slope).astype(BF16), (hidden_grad * activated).astype(BF16)], 1
    )


def store_branch(grads, inputs, weights, units, outs):
    branch = lax.dot_general(
        grads, weights[0][...], (((1,), (1,)), ((), ())), preferred_element_type=F32
    )
    unit_rows, root_mean = normalized(inputs)
    centered = branch - unit_rows * jnp.mean(branch * unit_rows, axis=-1, keepdims=True)
    rows = (centered / root_mean).astype(BF16)
    group = rows.shape[0] // SIDE
    for i, out in enumerate(outs):
        out[...] = rows[i * group : (i + 1) * group]


def started(copies):
    for copy in copies:
        copy.start()
    return copies


def waited(copies):
    for copy in copies:
        copy.wait()


def weight_copies(pieces, weights, sems):
    rows, columns = pieces[0].shape[0], weights.shape[1]
    first = pieces[0].shape[1] - columns
    return started(
        [
            pltpu.make_async_copy(
                piece.at[:, pl.ds(first, columns)], weights.at[pl.ds(i * rows, rows)], sems.at[i]
            )
            for i, piece in enumerate(pieces)
        ]
    )


def apart(weights, units):
    return weights.at[:, pl.ds(0, 2 * units)], weights.at[:, pl.ds(2 * units, units)]


def order_kernel(first, mover, whole, out, matrix, weights, sems):
    count = sems.shape[0] - 1
    columns = out.shape[1] // count
    copies = [pltpu.make_async_copy(mover, matrix, sems.at[0])]
    for i in range(count):
        source = whole.at[:, pl.ds(first + i * columns, columns)]
        target = weights.at[:, pl.ds(i * columns, columns)]
        copies.append(pltpu.make_async_copy(source, target, sems.at[i + 1]))
    started(copies)
    copies[0].wait()
    for i in range(count):
        copies[i + 1].wait()
        part = slice(i * columns, (i + 1) * columns)
        out[:, part] = dot(matrix[...], weights[:, part]).astype(BF16)


def gate_kernel(units, x, weights, *outs):
    normed = normalized(x[...])[0].astype(BF16)
    outs[0][...] = normed.T
    outs[1][...], outs[2][...], outs[3][...] = gate_parts(normed, (weights,), units)


def first_kernel(units, x, d, *refs):
    pieces, halves, outs = refs[:4], refs[4:8], refs[8:12]
    weights, sems, stages, out_sems = refs[12], refs[13], refs[14:18], refs[18]
    copies = weight_copies(pieces, weights, sems)
    weights = apart(weights, units)
    sends = [
        pltpu.make_async_copy(stage, half, out_sems.at[i])
        for i, (stage, half) in enumerate(zip(stages, halves))
    ]
    normed = normalized(x[...])[0].astype(BF16)
    stages[0][...] = normed.T
    sends[0].start()
    waited(copies)
    hidden, slope, activated = gate_parts(normed, weights, units)
    stages[1][...], stages[2][...], stages[3][...] = hidden, slope, activated
    started(sends[1:])
    grads = both_grads(d[...], slope, activated, weights, units)
    store_branch(grads, x[...], weights, units, outs)
    waited(sends)


def chain_kernel(units, active, x, slope, activated, ins, down, *refs):
    groups, outs = refs[:4], refs[4:]

    @pl.when(active[0] != 0)
    def _():
        cotangent = jnp.concatenate([g[...] for g in groups], 0)
        grads = both_grads(cotangent, slope[...], activated[...], (ins, down), units)
        store_branch(grads, x[...], (ins, down), units, outs)

    @pl.when(active[0] == 0)
    def _():
        for out in outs:
            out[...] = jnp.zeros(out.shape, out.dtype)


def far_chain_kernel(units, active, x, slope, activated, *refs):
    pieces, groups, outs = refs[:4], refs[4:8], refs[8:12]
    weights, sems, slope_here, activated_here = refs[12:]

    @pl.when(active[0] != 0)
    def _():
        copies = weight_copies(pieces, weights, sems)
        copies += started(
            [
                pltpu.make_async_copy(slope, slope_here, sems.at[4]),
                pltpu.make_async_copy(activated, activated_here, sems.at[5]),
            ]
        )
        cotangent = jnp.concatenate([g[...] for g in groups], 0)
        waited(copies)
        grads = both_grads(cotangent, slope_here[...], activated_here[...], apart(weights, units), units)
        store_branch(grads, x[...], apart(weights, units), units, outs)

    @pl.when(active[0] == 0)
    def _():
        for out in outs:
            out[...] = jnp.zeros(out.shape, out.dtype)


def early_kernel(units, x, d, *refs):
    if len(refs) > 6:
        pieces, outs, weights, sems = refs[:4], refs[4:8], refs[8], refs[9]
        copies, weights = weight_copies(pieces, weights, sems), apart(weights, units)
    else:
        weights, outs, copies = refs[:2], refs[2:], []
    normed = normalized(x[...])[0].astype(BF16)
    outs[0][...] = normed.T
    outs[1][...] = d[...].T
    waited(copies)
    hidden, slope, activated = gate_parts(normed, weights, units)
    outs[2][...] = hidden
    outs[3][...] = both_grads(d[...], slope, activated, weights, units)


def terms_kernel(units, use_first, *refs):
    first, second = refs[:4], refs[4:8]
    normed_early, cot_early, hidden_early, grads_early = refs[8:12]
    normed_last, hidden_last, slope, activated = refs[12:16]
    lefts, grads, hiddens = refs[-3:]
    if len(refs) > 24:
        pieces, outs, weights, sems = refs[16:20], refs[20:24], refs[24], refs[25]
        copies = weight_copies(pieces, weights, sems)
    else:
        weights, outs, copies = refs[16], refs[17:21], []
    tokens = normed_early.shape[1]
    cotangent = jnp.concatenate(
        [jnp.where(use_first[0] != 0, a[...], b[...]) for a, b in zip(first, second)], 0
    )
    lefts[0, :, :tokens] = normed_early[...]
    lefts[0, :, tokens:] = normed_last[...]
    lefts[1, :, :tokens] = cot_early[...]
    lefts[1, :, tokens:] = cotangent.T
    grads[:tokens] = grads_early[...]
    hiddens[:tokens] = hidden_early[...]
    hiddens[tokens:] = hidden_last[...]
    waited(copies)
    hidden_grad = dot(cotangent, weights[...])
    grads[tokens:, :units] = (hidden_grad * slope[...]).astype(BF16)
    grads[tokens:, units:] = (hidden_grad * activated[...]).astype(BF16)
    for i, out in enumerate(outs):
        rows = slice(i * out.shape[0], (i + 1) * out.shape[0])
        out[:, : 2 * units] = dot(lefts[0, rows], grads[...]).astype(BF16)
        out[:, 2 * units :] = dot(lefts[1, rows], hiddens[...]).astype(BF16)


def mix_kernel(crossing, d, *refs):
    total = d[...].astype(F32) + total_of([r[...] for r in refs[:4]])
    rows = total.astype(BF16)
    if crossing:
        rows = dot(rows, refs[4][...]).astype(BF16)
    refs[-1][...] = rows


def add_kernel(*refs):
    total = total_of([r[...] for r in refs[:4]])
    outs = refs[4:]
    rows = total.shape[0] // len(outs)
    for i, out in enumerate(outs):
        out[...] = total[i * rows : (i + 1) * rows].astype(out.dtype)


def finish_kernel(*refs):
    total = total_of([r[...] for r in refs[:4]])
    refs[4][...] = total
    squares = jnp.sum(total * total, axis=0, keepdims=True)
    refs[5][...] = jnp.broadcast_to(jnp.sum(squares, axis=1, keepdims=True), refs[5].shape)


def near_pieces(pieces):
    return {by: from_plane(pieces[by], -by, False) for by in (1, 3)}


def far_piece(piece):
    return {2: from_plane(piece, -2, False)}


def add_pieces(own, got):
    share, wide = own.shape[0] // SIDE, own.shape[1]
    outs = [((share, wide), F32)] + [((share, wide), BF16)] * 3
    return run(add_kernel, [own, got[1], got[2], got[3]], outs, name="add")


def own_rows(sums):
    parts = [sums[0]] + peers(lambda by: from_plane(sums[by], -by, True))
    return run(finish_kernel, parts, [(sums[0].shape, F32), ((8, 128), F32)], name="finish")


def reduced_group(first_group, got, matrix):
    return run(
        functools.partial(mix_kernel, matrix is not None),
        [first_group] + got + ([] if matrix is None else [matrix]),
        [(first_group.shape, BF16)],
        name="mix",
    )[0]


def scattered(parts):
    return [parts[0]] + peers(lambda by: from_z(parts[by], -by))


def shared_groups(mine):
    return [mine] + peers(lambda by: from_z(mine, by))


def summed_everywhere(value):
    value = value + from_other_core(value)
    value = total_of([value] + peers(lambda by: from_plane(value, by, True)))
    value = total_of([value] + peers(lambda by: from_plane(value, by, False)))
    return total_of([value] + peers(lambda by: from_z(value, by)))[0, 0]


def per_device(
    saved_inputs,
    early_cotangents,
    final_cotangent,
    valid_counts,
    master,
    first_moment,
    second_moment,
):
    tokens, width = saved_inputs.shape[3:]
    units = master.shape[4]
    share = width // lax.axis_size("dp")
    section = lax.axis_index("pipe")
    place = lax.axis_index("dp")
    place_y, place_x = place // SIDE, place % SIDE
    place_z = lax.axis_index("tensor")
    group = tokens // SIDE
    wide = 3 * units
    on_first = (section == 0).astype(jnp.int32).reshape(1)
    on_second = 1 - on_first

    def as_stored(array):
        return array[0].transpose(0, 2, 1, 3)

    masters = as_stored(master)

    def shard_of(leg):
        return masters[:, :, leg, :].astype(BF16).reshape(share, wide)

    shard = shard_of(1)
    block = jnp.concatenate([shard] + peers(lambda by: from_plane(shard, by, True)), 0)
    upper = [block] + peers(lambda by: from_plane(block, by, False))
    saved_inputs, early_cotangents, final_cotangent = after(
        (saved_inputs, early_cotangents, final_cotangent), block
    )

    block = jnp.arange(width) // share
    outer, inner = block // SIDE, block % SIDE
    by_y = jnp.where(section == 0, outer, inner)
    by_x = jnp.where(section == 0, inner, outer)
    source_block = ((place_y + by_y) % SIDE) * SIDE + (place_x + by_x) % SIDE
    source_column = source_block * share + jnp.arange(width) % share
    mover = (jnp.arange(width)[:, None] == source_column[None, :]).astype(BF16)
    swapped_column = (inner * SIDE + outer) * share + jnp.arange(width) % share
    swap = (jnp.arange(width)[:, None] == swapped_column[None, :]).astype(BF16)
    turns = [(place_z + j) % SIDE for j in range(SIDE)]

    def turned(rows):
        return jnp.concatenate(
            [lax.dynamic_slice_in_dim(rows, turn * group, group, rows.ndim - 2) for turn in turns],
            rows.ndim - 2,
        )

    def moved(rows):
        return jnp.dot(turned(rows), mover, preferred_element_type=F32).astype(BF16)

    inputs = moved(saved_inputs[0])
    position = turned(lax.broadcasted_iota(jnp.int32, (tokens, 1), 0))
    early = jnp.where(position < valid_counts[0, 0], moved(early_cotangents[0]), 0)
    final = jnp.where(position < valid_counts[0, 1], moved(final_cotangent), 0)
    lower_whole = lax.all_gather(after(shard_of(0), final), "dp", axis=0, tiled=True)
    final_groups = [final[i * group : (i + 1) * group] for i in range(SIDE)]

    flop = 2 * tokens * width * units
    half_outs = [
        ((width, tokens), BF16),
        ((tokens, units), BF16),
        ((tokens, units), F32),
        ((tokens, units), F32),
    ]
    group_outs = [((group, width), BF16)] * SIDE

    def far(arrays):
        return [(array, pltpu.HBM) for array in arrays]

    def fetched(columns):
        return [pltpu.VMEM((width, columns), BF16), pltpu.SemaphoreType.DMA((6,))]

    def early_parts(leg, leg_inputs, weights):
        one = len(weights) < 4
        return run(
            functools.partial(early_kernel, units),
            [leg_inputs, early[leg], *(weights if one else far(weights))],
            [
                ((width, tokens), BF16),
                ((width, tokens), BF16),
                ((tokens, units), BF16),
                ((tokens, 2 * units), BF16),
            ],
            [] if one else fetched(wide),
            5 * flop,
            "early",
        )

    def terms(use_first, first, second, early_half, half, weights):
        one = len(weights) < 4
        return run(
            functools.partial(terms_kernel, units),
            [
                (use_first, pltpu.SMEM),
                *first,
                *second,
                *early_half,
                *half,
                *(weights if one else far(weights)),
            ],
            [((width // SIDE, wide), BF16)] * SIDE,
            ([] if one else fetched(units))
            + [
                pltpu.VMEM((2, width, 2 * tokens), BF16),
                pltpu.VMEM((2 * tokens, 2 * units), BF16),
                pltpu.VMEM((2 * tokens, units), BF16),
            ],
            7 * flop,
            "terms",
        )

    upper = after(upper, (inputs, early, final, mover))
    outs = run(
        functools.partial(first_kernel, units),
        [inputs[1, 1], final, *far(upper)],
        [(*out, pltpu.HBM) for out in half_outs] + group_outs,
        fetched(wide)
        + [pltpu.VMEM(*out) for out in half_outs]
        + [pltpu.SemaphoreType.DMA((SIDE,))],
        5 * flop,
        "first",
    )
    upper_half, part3 = outs[:4], outs[4:]
    got = scattered(part3)
    early_one = early_parts(1, after(inputs[1, 0], part3[0]), upper)
    mine2 = reduced_group(after(final_groups[0], early_one), got, swap)
    cot2 = [across(mine2, by, 0) for by in range(SIDE)]
    part2 = run(
        functools.partial(far_chain_kernel, units),
        [
            (on_second, pltpu.SMEM),
            inputs[1, 1],
            *far(upper_half[2:]),
            *far(upper),
            *cot2,
        ],
        group_outs,
        fetched(wide) + [pltpu.VMEM(*out) for out in half_outs[2:]],
        3 * flop,
        "chain",
    )

    got = [across(part2[by], -by, 1) for by in range(SIDE)]

    def ordered(columns, count, *others):
        first, last = columns
        return run(
            functools.partial(order_kernel, first),
            far([mover.T, after(lower_whole, *others)]),
            [((width, last - first), BF16)],
            [
                pltpu.VMEM((width, width), BF16),
                pltpu.VMEM((width, last - first), BF16),
                pltpu.SemaphoreType.DMA((count + 1,)),
            ],
            2 * width * width * (last - first),
            "order",
        )[0]

    lower_ins = ordered((0, 2 * units), 2, part2[0])
    mine1 = reduced_group(after(mine2, lower_ins), got, None)
    cot1 = [across(mine1, by, 0) for by in range(SIDE)]
    lower_half = run(
        functools.partial(gate_kernel, units),
        [after(inputs[0, 1], mine1), lower_ins],
        half_outs,
        flops=2 * flop,
        name="gate",
    )
    lower_down = ordered((2 * units, 3 * units), 1, mine1)
    part1 = run(
        functools.partial(chain_kernel, units),
        [
            (on_second, pltpu.SMEM),
            inputs[0, 1],
            lower_half[2],
            lower_half[3],
            lower_ins,
            lower_down,
            *cot1,
        ],
        group_outs,
        flops=3 * flop,
        name="chain",
    )
    got = [across(part1[by], -by, 1) for by in range(SIDE)]
    early_one = after(early_one, part1[0])
    upper_terms = terms(on_first, final_groups, cot2, early_one, upper_half, upper)
    mine0 = reduced_group(after(mine1, upper_terms[0]), got, swap)
    cot0 = shared_groups(mine0)
    upper_got = near_pieces(after(upper_terms, mine0))
    early_zero = early_parts(0, after(inputs[0, 0], mine0), [lower_ins, lower_down])
    upper_got |= far_piece(after(upper_terms[2], cot0))
    early_zero = after(early_zero, [upper_got[by] for by in (1, 3)])
    lower_terms = terms(on_second, cot1, cot0, early_zero, lower_half, [lower_down])

    lower_got = near_pieces(lower_terms) | far_piece(lower_terms[2])
    upper_sums = add_pieces(after(upper_terms[0], lower_terms[0]), upper_got)
    upper_gradient, upper_squares = own_rows(upper_sums)
    lower_gradient, lower_squares = own_rows(add_pieces(lower_terms[0], lower_got))
    gradient = jnp.stack(
        [rows.reshape(share, 3, units) for rows in (lower_gradient, upper_gradient)], 2
    )

    total = summed_everywhere(lower_squares + upper_squares)
    param_count = lax.axis_size("pipe") * 6 * width * units * lax.axis_size("tensor")
    clip_factor = jnp.minimum(1.0, math.sqrt(param_count) / (jnp.sqrt(total) + 1e-06))
    scaled = gradient * clip_factor
    moment_one = 0.9 * as_stored(first_moment).astype(F32) + 0.1 * scaled
    moment_two = 0.95 * as_stored(second_moment).astype(F32) + 0.05 * scaled * scaled
    update = (
        moment_one / (1.0 - 0.9**STEP) / (jnp.sqrt(moment_two / (1.0 - 0.95**STEP)) + 1e-08)
        + 0.1 * masters
    )
    results = (masters - 0.001 * update, moment_one.astype(BF16), moment_two.astype(BF16))
    return tuple(result.transpose(0, 2, 1, 3)[None] for result in results)


def solution(mesh):
    in_specs = (
        P("pipe", None, None, "dp", None),
        P("pipe", None, "dp", None),
        P("dp", None),
        P("dp", None),
        P("pipe", "dp", None, None, "tensor"),
        P("pipe", "dp", None, None, "tensor"),
        P("pipe", "dp", None, None, "tensor"),
    )
    out_specs = (
        P("pipe", "dp", None, None, "tensor"),
        P("pipe", "dp", None, None, "tensor"),
        P("pipe", "dp", None, None, "tensor"),
    )
    return jax.shard_map(
        per_device, mesh=mesh, in_specs=in_specs, out_specs=out_specs, check_vma=False
    )
```

```python
import functools
import math

import jax
import jax.numpy as jnp
from jax import lax
from jax.experimental import pallas as pl
from jax.experimental.pallas import tpu as pltpu
from jax.sharding import PartitionSpec as P

STEP = 20
SIDE = 4
F32 = jnp.float32
BF16 = jnp.bfloat16
ORDER = (1, 3, 2)
VMEM_LIMIT = 20 * 1024 * 1024


def peers(fetch):
    got = {by: fetch(by) for by in ORDER}
    return [got[by] for by in (1, 2, 3)]


def from_plane(value, by, first):
    pairs = []
    for core in range(2):
        for y in range(SIDE):
            for x in range(SIDE):
                if (core == 0) == first:
                    source = (y, (x + by) % SIDE)
                else:
                    source = ((y + by) % SIDE, x)
                base = core * SIDE * SIDE
                pairs.append((base + source[0] * SIDE + source[1], base + y * SIDE + x))
    return lax.ppermute(value, ("pipe", "dp"), pairs)


def from_z(value, by):
    pairs = [((z + by) % SIDE, z) for z in range(SIDE)]
    return lax.ppermute(value, "tensor", pairs)


def across(value, by, source):
    pairs = [(source * SIDE + (z + by) % SIDE, (1 - source) * SIDE + z) for z in range(SIDE)]
    pairs += [((1 - source) * SIDE + z, source * SIDE + z) for z in range(SIDE)]
    return lax.ppermute(value, ("pipe", "tensor"), pairs)


def from_other_core(value):
    return lax.ppermute(value, "pipe", [(0, 1), (1, 0)])


def total_of(parts):
    total = parts[0].astype(F32)
    for part in parts[1:]:
        total = total + part.astype(F32)
    return total


def run(kernel, ins, outs, scratch=(), flops=0, name=None, limit=VMEM_LIMIT):
    arrays, specs = [], []
    for item in ins:
        array, space = item if isinstance(item, tuple) else (item, pltpu.VMEM)
        arrays.append(array)
        specs.append(pl.BlockSpec(memory_space=space))
    moved = sum(a.size * a.dtype.itemsize for a in arrays)
    moved += sum(math.prod(o[0]) * jnp.dtype(o[1]).itemsize for o in outs)
    return pl.pallas_call(
        kernel,
        out_shape=[jax.ShapeDtypeStruct(o[0], o[1]) for o in outs],
        in_specs=specs,
        out_specs=[pl.BlockSpec(memory_space=o[2] if o[2:] else pltpu.VMEM) for o in outs],
        scratch_shapes=list(scratch),
        compiler_params=pltpu.CompilerParams(vmem_limit_bytes=limit),
        cost_estimate=pl.CostEstimate(flops=flops, bytes_accessed=moved, transcendentals=0),
        name=name,
    )(*arrays)


def after(value, *others):
    return lax.optimization_barrier((value, others))[0]


def normalized(inputs):
    values = inputs.astype(F32)
    root_mean = jnp.sqrt(jnp.mean(values * values, axis=-1, keepdims=True) + 1e-06)
    return values / root_mean, root_mean


def dot(left, right):
    return jnp.dot(left, right, preferred_element_type=F32)


def gate_parts(normed, weights, units):
    both = dot(normed, weights[0][...])
    gate, up_rows = both[:, :units], both[:, units:]
    sigmoid_gate = jax.nn.sigmoid(gate)
    activated = gate * sigmoid_gate
    hidden = (activated * up_rows).astype(BF16)
    slope = up_rows * sigmoid_gate * (1.0 + gate * (1.0 - sigmoid_gate))
    return hidden, slope, activated


def both_grads(cotangent, slope, activated, weights, units):
    hidden_grad = dot(cotangent, weights[1][...])
    return jnp.concatenate(
        [(hidden_grad * slope).astype(BF16), (hidden_grad * activated).astype(BF16)], 1
    )


def store_branch(grads, inputs, weights, units, outs):
    branch = lax.dot_general(
        grads, weights[0][...], (((1,), (1,)), ((), ())), preferred_element_type=F32
    )
    unit_rows, root_mean = normalized(inputs)
    centered = branch - unit_rows * jnp.mean(branch * unit_rows, axis=-1, keepdims=True)
    rows = (centered / root_mean).astype(BF16)
    group = rows.shape[0] // SIDE
    for i, out in enumerate(outs):
        out[...] = rows[i * group : (i + 1) * group]


def started(copies):
    for copy in copies:
        copy.start()
    return copies


def waited(copies):
    for copy in copies:
        copy.wait()


def weight_copies(pieces, weights, sems):
    rows, columns = pieces[0].shape[0], weights.shape[1]
    first = pieces[0].shape[1] - columns
    return started(
        [
            pltpu.make_async_copy(
                piece.at[:, pl.ds(first, columns)], weights.at[pl.ds(i * rows, rows)], sems.at[i]
            )
            for i, piece in enumerate(pieces)
        ]
    )


def apart(weights, units):
    return weights.at[:, pl.ds(0, 2 * units)], weights.at[:, pl.ds(2 * units, units)]


def order_kernel(first, mover, whole, out, matrix, weights, sems):
    count = sems.shape[0] - 1
    columns = out.shape[1] // count
    copies = [pltpu.make_async_copy(mover, matrix, sems.at[0])]
    for i in range(count):
        source = whole.at[:, pl.ds(first + i * columns, columns)]
        target = weights.at[:, pl.ds(i * columns, columns)]
        copies.append(pltpu.make_async_copy(source, target, sems.at[i + 1]))
    started(copies)
    copies[0].wait()
    for i in range(count):
        copies[i + 1].wait()
        part = slice(i * columns, (i + 1) * columns)
        out[:, part] = dot(matrix[...], weights[:, part]).astype(BF16)


def gate_kernel(units, x, weights, *outs):
    normed = normalized(x[...])[0].astype(BF16)
    outs[0][...] = normed.T
    outs[1][...], outs[2][...], outs[3][...] = gate_parts(normed, (weights,), units)


def first_kernel(units, x, d, *refs):
    pieces, halves, outs = refs[:4], refs[4:8], refs[8:12]
    weights, sems, stages, out_sems = refs[12], refs[13], refs[14:18], refs[18]
    copies = weight_copies(pieces, weights, sems)
    weights = apart(weights, units)
    sends = [
        pltpu.make_async_copy(stage, half, out_sems.at[i])
        for i, (stage, half) in enumerate(zip(stages, halves))
    ]
    normed = normalized(x[...])[0].astype(BF16)
    stages[0][...] = normed.T
    sends[0].start()
    waited(copies)
    hidden, slope, activated = gate_parts(normed, weights, units)
    stages[1][...], stages[2][...], stages[3][...] = hidden, slope, activated
    started(sends[1:])
    grads = both_grads(d[...], slope, activated, weights, units)
    store_branch(grads, x[...], weights, units, outs)
    waited(sends)


def chain_kernel(units, active, x, slope, activated, ins, down, *refs):
    groups, outs = refs[:4], refs[4:]

    @pl.when(active[0] != 0)
    def _():
        cotangent = jnp.concatenate([g[...] for g in groups], 0)
        grads = both_grads(cotangent, slope[...], activated[...], (ins, down), units)
        store_branch(grads, x[...], (ins, down), units, outs)

    @pl.when(active[0] == 0)
    def _():
        for out in outs:
            out[...] = jnp.zeros(out.shape, out.dtype)


def far_chain_kernel(units, active, x, slope, activated, *refs):
    pieces, groups, outs = refs[:4], refs[4:8], refs[8:12]
    weights, sems, slope_here, activated_here = refs[12:]

    @pl.when(active[0] != 0)
    def _():
        copies = weight_copies(pieces, weights, sems)
        copies += started(
            [
                pltpu.make_async_copy(slope, slope_here, sems.at[4]),
                pltpu.make_async_copy(activated, activated_here, sems.at[5]),
            ]
        )
        cotangent = jnp.concatenate([g[...] for g in groups], 0)
        waited(copies)
        grads = both_grads(cotangent, slope_here[...], activated_here[...], apart(weights, units), units)
        store_branch(grads, x[...], apart(weights, units), units, outs)

    @pl.when(active[0] == 0)
    def _():
        for out in outs:
            out[...] = jnp.zeros(out.shape, out.dtype)


def early_kernel(units, x, d, *refs):
    if len(refs) > 6:
        pieces, outs, weights, sems = refs[:4], refs[4:8], refs[8], refs[9]
        copies, weights = weight_copies(pieces, weights, sems), apart(weights, units)
    else:
        weights, outs, copies = refs[:2], refs[2:], []
    normed = normalized(x[...])[0].astype(BF16)
    outs[0][...] = normed.T
    outs[1][...] = d[...].T
    waited(copies)
    hidden, slope, activated = gate_parts(normed, weights, units)
    outs[2][...] = hidden
    outs[3][...] = both_grads(d[...], slope, activated, weights, units)


def terms_kernel(units, use_first, *refs):
    first, second = refs[:4], refs[4:8]
    normed_early, cot_early, hidden_early, grads_early = refs[8:12]
    normed_last, hidden_last, slope, activated = refs[12:16]
    lefts, grads, hiddens = refs[-3:]
    if len(refs) > 24:
        pieces, outs, weights, sems = refs[16:20], refs[20:24], refs[24], refs[25]
        copies = weight_copies(pieces, weights, sems)
    else:
        weights, outs, copies = refs[16], refs[17:21], []
    tokens = normed_early.shape[1]
    cotangent = jnp.concatenate(
        [jnp.where(use_first[0] != 0, a[...], b[...]) for a, b in zip(first, second)], 0
    )
    lefts[0, :, :tokens] = normed_early[...]
    lefts[0, :, tokens:] = normed_last[...]
    lefts[1, :, :tokens] = cot_early[...]
    lefts[1, :, tokens:] = cotangent.T
    grads[:tokens] = grads_early[...]
    hiddens[:tokens] = hidden_early[...]
    hiddens[tokens:] = hidden_last[...]
    waited(copies)
    hidden_grad = dot(cotangent, weights[...])
    grads[tokens:, :units] = (hidden_grad * slope[...]).astype(BF16)
    grads[tokens:, units:] = (hidden_grad * activated[...]).astype(BF16)
    for i, out in enumerate(outs):
        rows = slice(i * out.shape[0], (i + 1) * out.shape[0])
        out[:, : 2 * units] = dot(lefts[0, rows], grads[...]).astype(BF16)
        out[:, 2 * units :] = dot(lefts[1, rows], hiddens[...]).astype(BF16)


def mix_kernel(crossing, d, *refs):
    total = d[...].astype(F32) + total_of([r[...] for r in refs[:4]])
    rows = total.astype(BF16)
    if crossing:
        rows = dot(rows, refs[4][...]).astype(BF16)
    refs[-1][...] = rows


def add_kernel(*refs):
    total = total_of([r[...] for r in refs[:4]])
    outs = refs[4:]
    rows = total.shape[0] // len(outs)
    for i, out in enumerate(outs):
        out[...] = total[i * rows : (i + 1) * rows].astype(out.dtype)


def finish_kernel(*refs):
    total = total_of([r[...] for r in refs[:4]])
    refs[4][...] = total
    squares = jnp.sum(total * total, axis=0, keepdims=True)
    refs[5][...] = jnp.broadcast_to(jnp.sum(squares, axis=1, keepdims=True), refs[5].shape)


def near_pieces(pieces):
    return {by: from_plane(pieces[by], -by, False) for by in (1, 3)}


def far_piece(piece):
    return {2: from_plane(piece, -2, False)}


def add_pieces(own, got):
    share, wide = own.shape[0] // SIDE, own.shape[1]
    outs = [((share, wide), F32)] + [((share, wide), BF16)] * 3
    return run(add_kernel, [own, got[1], got[2], got[3]], outs, name="add")


def own_rows(sums):
    parts = [sums[0]] + peers(lambda by: from_plane(sums[by], -by, True))
    return run(finish_kernel, parts, [(sums[0].shape, F32), ((8, 128), F32)], name="finish")


def reduced_group(first_group, got, matrix):
    return run(
        functools.partial(mix_kernel, matrix is not None),
        [first_group] + got + ([] if matrix is None else [matrix]),
        [(first_group.shape, BF16)],
        name="mix",
    )[0]


def scattered(parts):
    return [parts[0]] + peers(lambda by: from_z(parts[by], -by))


def shared_groups(mine):
    return [mine] + peers(lambda by: from_z(mine, by))


def summed_everywhere(value):
    value = value + from_other_core(value)
    value = total_of([value] + peers(lambda by: from_plane(value, by, True)))
    value = total_of([value] + peers(lambda by: from_plane(value, by, False)))
    return total_of([value] + peers(lambda by: from_z(value, by)))[0, 0]


def per_device(
    saved_inputs,
    early_cotangents,
    final_cotangent,
    valid_counts,
    master,
    first_moment,
    second_moment,
):
    tokens, width = saved_inputs.shape[3:]
    units = master.shape[4]
    share = width // lax.axis_size("dp")
    section = lax.axis_index("pipe")
    place = lax.axis_index("dp")
    place_y, place_x = place // SIDE, place % SIDE
    place_z = lax.axis_index("tensor")
    group = tokens // SIDE
    wide = 3 * units
    on_first = (section == 0).astype(jnp.int32).reshape(1)
    on_second = 1 - on_first

    def as_stored(array):
        return array[0].transpose(0, 2, 1, 3)

    masters = as_stored(master)

    def shard_of(leg):
        return masters[:, :, leg, :].astype(BF16).reshape(share, wide)

    shard = shard_of(1)
    block = jnp.concatenate([shard] + peers(lambda by: from_plane(shard, by, True)), 0)
    lower_whole = lax.all_gather(shard_of(0), "dp", axis=0, tiled=True)
    upper = [block] + peers(lambda by: from_plane(block, by, False))
    saved_inputs, early_cotangents, final_cotangent = after(
        (saved_inputs, early_cotangents, final_cotangent), block
    )

    block = jnp.arange(width) // share
    outer, inner = block // SIDE, block % SIDE
    by_y = jnp.where(section == 0, outer, inner)
    by_x = jnp.where(section == 0, inner, outer)
    source_block = ((place_y + by_y) % SIDE) * SIDE + (place_x + by_x) % SIDE
    source_column = source_block * share + jnp.arange(width) % share
    mover = (jnp.arange(width)[:, None] == source_column[None, :]).astype(BF16)
    swapped_column = (inner * SIDE + outer) * share + jnp.arange(width) % share
    swap = (jnp.arange(width)[:, None] == swapped_column[None, :]).astype(BF16)
    turns = [(place_z + j) % SIDE for j in range(SIDE)]

    def turned(rows):
        return jnp.concatenate(
            [lax.dynamic_slice_in_dim(rows, turn * group, group, rows.ndim - 2) for turn in turns],
            rows.ndim - 2,
        )

    def moved(rows):
        return jnp.dot(turned(rows), mover, preferred_element_type=F32).astype(BF16)

    inputs = moved(saved_inputs[0])
    position = turned(lax.broadcasted_iota(jnp.int32, (tokens, 1), 0))
    early = jnp.where(position < valid_counts[0, 0], moved(early_cotangents[0]), 0)
    final = jnp.where(position < valid_counts[0, 1], moved(final_cotangent), 0)
    final_groups = [final[i * group : (i + 1) * group] for i in range(SIDE)]

    flop = 2 * tokens * width * units
    half_outs = [
        ((width, tokens), BF16),
        ((tokens, units), BF16),
        ((tokens, units), F32),
        ((tokens, units), F32),
    ]
    group_outs = [((group, width), BF16)] * SIDE

    def far(arrays):
        return [(array, pltpu.HBM) for array in arrays]

    def fetched(columns):
        return [pltpu.VMEM((width, columns), BF16), pltpu.SemaphoreType.DMA((6,))]

    def early_parts(leg, leg_inputs, weights):
        one = len(weights) < 4
        return run(
            functools.partial(early_kernel, units),
            [leg_inputs, early[leg], *(weights if one else far(weights))],
            [
                ((width, tokens), BF16),
                ((width, tokens), BF16),
                ((tokens, units), BF16),
                ((tokens, 2 * units), BF16),
            ],
            [] if one else fetched(wide),
            5 * flop,
            "early",
        )

    def terms(use_first, first, second, early_half, half, weights):
        one = len(weights) < 4
        return run(
            functools.partial(terms_kernel, units),
            [
                (use_first, pltpu.SMEM),
                *first,
                *second,
                *early_half,
                *half,
                *(weights if one else far(weights)),
            ],
            [((width // SIDE, wide), BF16)] * SIDE,
            ([] if one else fetched(units))
            + [
                pltpu.VMEM((2, width, 2 * tokens), BF16),
                pltpu.VMEM((2 * tokens, 2 * units), BF16),
                pltpu.VMEM((2 * tokens, units), BF16),
            ],
            7 * flop,
            "terms",
        )

    upper = after(upper, (inputs, early, final, mover))
    outs = run(
        functools.partial(first_kernel, units),
        [inputs[1, 1], final, *far(upper)],
        [(*out, pltpu.HBM) for out in half_outs] + group_outs,
        fetched(wide)
        + [pltpu.VMEM(*out) for out in half_outs]
        + [pltpu.SemaphoreType.DMA((SIDE,))],
        5 * flop,
        "first",
    )
    upper_half, part3 = outs[:4], outs[4:]
    got = scattered(part3)
    early_one = early_parts(1, after(inputs[1, 0], part3[0]), upper)
    mine2 = reduced_group(after(final_groups[0], early_one), got, swap)
    cot2 = [across(mine2, by, 0) for by in range(SIDE)]
    part2 = run(
        functools.partial(far_chain_kernel, units),
        [
            (on_second, pltpu.SMEM),
            inputs[1, 1],
            *far(upper_half[2:]),
            *far(upper),
            *cot2,
        ],
        group_outs,
        fetched(wide) + [pltpu.VMEM(*out) for out in half_outs[2:]],
        3 * flop,
        "chain",
    )

    got = [across(part2[by], -by, 1) for by in range(SIDE)]

    def ordered(columns, count, *others):
        first, last = columns
        return run(
            functools.partial(order_kernel, first),
            far([mover.T, after(lower_whole, *others)]),
            [((width, last - first), BF16)],
            [
                pltpu.VMEM((width, width), BF16),
                pltpu.VMEM((width, last - first), BF16),
                pltpu.SemaphoreType.DMA((count + 1,)),
            ],
            2 * width * width * (last - first),
            "order",
        )[0]

    lower_ins = ordered((0, 2 * units), 2, part2[0])
    mine1 = reduced_group(after(mine2, lower_ins), got, None)
    cot1 = [across(mine1, by, 0) for by in range(SIDE)]
    lower_half = run(
        functools.partial(gate_kernel, units),
        [after(inputs[0, 1], mine1), lower_ins],
        half_outs,
        flops=2 * flop,
        name="gate",
    )
    lower_down = ordered((2 * units, 3 * units), 1, mine1)
    part1 = run(
        functools.partial(chain_kernel, units),
        [
            (on_second, pltpu.SMEM),
            inputs[0, 1],
            lower_half[2],
            lower_half[3],
            lower_ins,
            lower_down,
            *cot1,
        ],
        group_outs,
        flops=3 * flop,
        name="chain",
    )
    got = [across(part1[by], -by, 1) for by in range(SIDE)]
    early_one = after(early_one, part1[0])
    upper_terms = terms(on_first, final_groups, cot2, early_one, upper_half, upper)
    mine0 = reduced_group(after(mine1, upper_terms[0]), got, swap)
    cot0 = shared_groups(mine0)
    upper_got = near_pieces(after(upper_terms, mine0))
    early_zero = early_parts(0, after(inputs[0, 0], mine0), [lower_ins, lower_down])
    early_zero = after(early_zero, [upper_got[by] for by in (1, 3)])
    lower_terms = terms(on_second, cot1, cot0, early_zero, lower_half, [lower_down])
    upper_got |= far_piece(after(upper_terms[2], lower_terms[0]))

    lower_got = near_pieces(lower_terms) | far_piece(lower_terms[2])
    upper_sums = add_pieces(after(upper_terms[0], lower_terms[0]), upper_got)
    upper_gradient, upper_squares = own_rows(upper_sums)
    lower_gradient, lower_squares = own_rows(add_pieces(lower_terms[0], lower_got))
    gradient = jnp.stack(
        [rows.reshape(share, 3, units) for rows in (lower_gradient, upper_gradient)], 2
    )

    total = summed_everywhere(lower_squares + upper_squares)
    param_count = lax.axis_size("pipe") * 6 * width * units * lax.axis_size("tensor")
    clip_factor = jnp.minimum(1.0, math.sqrt(param_count) / (jnp.sqrt(total) + 1e-06))
    scaled = gradient * clip_factor
    moment_one = 0.9 * as_stored(first_moment).astype(F32) + 0.1 * scaled
    moment_two = 0.95 * as_stored(second_moment).astype(F32) + 0.05 * scaled * scaled
    update = (
        moment_one / (1.0 - 0.9**STEP) / (jnp.sqrt(moment_two / (1.0 - 0.95**STEP)) + 1e-08)
        + 0.1 * masters
    )
    results = (masters - 0.001 * update, moment_one.astype(BF16), moment_two.astype(BF16))
    return tuple(result.transpose(0, 2, 1, 3)[None] for result in results)


def solution(mesh):
    in_specs = (
        P("pipe", None, None, "dp", None),
        P("pipe", None, "dp", None),
        P("dp", None),
        P("dp", None),
        P("pipe", "dp", None, None, "tensor"),
        P("pipe", "dp", None, None, "tensor"),
        P("pipe", "dp", None, None, "tensor"),
    )
    out_specs = (
        P("pipe", "dp", None, None, "tensor"),
        P("pipe", "dp", None, None, "tensor"),
        P("pipe", "dp", None, None, "tensor"),
    )
    return jax.shard_map(
        per_device, mesh=mesh, in_specs=in_specs, out_specs=out_specs, check_vma=False
    )
```
